512 devices in a mesh: sky: 16 (over y_lo, x, core), uv: 32 (over z, y_hi).
Axes of the slice: x: 4, y: 8 (y_hi: 4, y_lo: 2; y = y_hi * 2 + y_lo), z: 8, core: 2. Of those that a mesh axis runs over, the one named last changes fastest.
Arguments:
- sky_model: bfloat16 [64, 256, 256], P('sky'), may hold values from -6 to 6
- beam: float32 [32, 4, 16, 2, 256], P('uv'), may hold values from 0.25 to 1
- tile_anchor: int32 [64, 2], replicated, may hold values from 0 to 63
- coverage: int32 [32, 16], P('uv'), may hold values from 0 to 63, as said below
- unit_chan: int32 [32, 16], P('uv'), may hold values from 0 to 3
- unit_block: int32 [32, 16, 2], P('uv'), may hold values from 0 to 63
- unit_occupied_mask: int32 [32, 16], P('uv'), may hold values 0 or 1
- observed: bfloat16 [32, 16, 2, 256, 256], P('uv', 'sky'), may hold values from -12 to 12
Outputs:
- residual_vis: bfloat16 [32, 16, 2, 256, 256], P('uv', 'sky')
- residual_image: bfloat16 [64, 256, 256], P('sky')
The draws below stay inside these ranges and needn't reach their ends.
Inputs may be any that keep to these rules, and one draw needn't show every extreme that they name: `coverage`: slot k of every pointing's list names one of the tiles of sky index k: a number from k * 4 to k * 4 + 3.
All inputs are finite; a program needn't handle non-finite values. No bound on the sum of `unit_occupied_mask` on one device may be relied on, other than what follows from the above.
Results may differ from the reference program's by a relative error of at most 0.02.
Values may be sent and summed in bfloat16 or wider, within the bound.
No kernel may reach another device: no remote copies, remote signals or barrier semaphores. Data moves between devices by JAX's collectives and lax.ppermute only.
A program may use at most 64 MiB of HBM per device.

```python
import math
import jax
import jax.numpy as jnp
from jax import lax

PIXELS = 256
GRID_TILES = 64
CHANNELS = 4
TILES_DEV = 4
TILES = 64
POINTINGS = 32
N_SKY = 16


def draw_coverage(key, part):
    key = jax.random.fold_in(key, 7)
    within = jax.random.randint(key, (POINTINGS, N_SKY), 0, TILES_DEV)
    within = within.at[0, 0].set(0)
    within = within.at[POINTINGS - 1, N_SKY - 1].set(TILES_DEV - 1)
    return (within + TILES_DEV * jnp.arange(N_SKY, dtype=jnp.int32)[None, :]).astype(jnp.int32)


def touch_ends(result, own_key, least, largest):
    longest = result.shape.index(max(result.shape))
    spots = []
    for shift in (0, 1):
        where = [jax.random.randint(jax.random.fold_in(own_key, axis), (), 0, length) for axis, length in enumerate(result.shape)]
        where[longest] = (where[longest] + shift) % result.shape[longest]
        spots.append(tuple(where))
    return result.at[spots[0]].set(least).at[spots[1]].set(largest)


def shard_levels(key, dims, cuts, least, largest):
    factor_of = 1.0
    for dim, parts in cuts:
        heights = jax.random.uniform(jax.random.fold_in(jax.random.fold_in(key, 6), dim), (parts,), jnp.float32, least / len(cuts), largest / len(cuts))
        factor_of = factor_of * jnp.repeat(jnp.exp(heights), dims[dim] // parts).reshape((-1,) + (1,) * (len(dims) - 1 - dim))
    return factor_of


def scatter_about(key, dims, spread, bound, split=(), kind=jnp.bfloat16):
    values = jax.random.normal(key, dims, jnp.float32) * spread
    if len(split) > 0:
        values = shard_levels(key, dims, split, -0.22, 0.18) * values
    return jnp.clip(values, min=-bound, max=bound).astype(kind)


def setup_inputs(seed: int = 0) -> dict:
    key_of = jax.random.split(jax.random.key(seed), 9)
    sky_model = scatter_about(key_of[0], (TILES, PIXELS, PIXELS), 1.0, 6.0, ((0, 16),))
    beam = jnp.clip(jnp.exp(math.log(1.0) - 1.3862944 * jax.random.uniform(key_of[1], (POINTINGS, CHANNELS, N_SKY, 2, PIXELS), jnp.float32) ** shard_levels(key_of[1], (POINTINGS, CHANNELS, N_SKY, 2, PIXELS), ((0, 32),), -0.2, 0.2)), 0.25, 1.0)
    tile_anchor = touch_ends(jax.random.randint(key_of[2], (TILES, 2), 0, GRID_TILES), jax.random.fold_in(key_of[2], 1), 0, GRID_TILES - 1).astype(jnp.int32)
    coverage = draw_coverage(jax.random.fold_in(key_of[8], 71), 0)
    unit_chan = touch_ends(jax.random.randint(key_of[4], (POINTINGS, N_SKY), 0, CHANNELS), jax.random.fold_in(key_of[4], 1), 0, CHANNELS - 1).astype(jnp.int32)
    unit_block = touch_ends(jax.random.randint(key_of[5], (POINTINGS, N_SKY, 2), 0, GRID_TILES), jax.random.fold_in(key_of[5], 1), 0, GRID_TILES - 1).astype(jnp.int32)
    unit_occupied_mask = touch_ends((jax.random.randint(key_of[6], (POINTINGS, N_SKY), 0, 2) < 1).astype(jnp.int32), jax.random.fold_in(key_of[6], 1), 0, 1)
    observed = scatter_about(key_of[7], (POINTINGS, N_SKY, 2, PIXELS, PIXELS), 2.0, 12.0, ((0, 32), (1, 16)))
    return {"sky_model": sky_model, "beam": beam, "tile_anchor": tile_anchor, "coverage": coverage, "unit_chan": unit_chan, "unit_block": unit_block, "unit_occupied_mask": unit_occupied_mask, "observed": observed}


def phase_tables(offset, anchor):
    counter = jnp.arange(PIXELS, dtype=jnp.int32)
    frequency = offset + GRID_TILES * counter
    coords = PIXELS * anchor + counter
    product = (frequency[:, None] * coords[None, :]) % (GRID_TILES * PIXELS)
    angles = product.astype(jnp.float32) * (2.0 * math.pi / (GRID_TILES * PIXELS))
    factor = PIXELS ** -0.5
    return ((jnp.cos(angles) * factor).astype(jnp.bfloat16), (jnp.sin(angles) * factor).astype(jnp.bfloat16))


def apply_beam(sky_tile, profiles):
    shaped = profiles[0][:, None] * profiles[1][None, :]
    return (sky_tile.astype(jnp.float32) * shaped).astype(jnp.bfloat16)


def predict(weighted, tables):
    cos_rows, sin_rows, cos_cols, sin_cols = tables
    stacked_cols = jnp.concatenate([cos_cols, sin_cols], axis=0)
    partial_rows = jnp.dot(weighted, stacked_cols.T, preferred_element_type=jnp.float32).astype(jnp.bfloat16)
    stacked_rows = jnp.concatenate([cos_rows, sin_rows], axis=0)
    blocks = jnp.dot(stacked_rows, partial_rows, preferred_element_type=jnp.float32)
    real_part = blocks[:PIXELS, :PIXELS] - blocks[PIXELS:, PIXELS:]
    imag_part = -(blocks[PIXELS:, :PIXELS] + blocks[:PIXELS, PIXELS:])
    return jnp.stack([real_part, imag_part])


def regrid(residual_value, tables):
    cos_rows, sin_rows, cos_cols, sin_cols = tables
    left_table = jnp.concatenate([jnp.concatenate([cos_rows, sin_rows], axis=1), jnp.concatenate([-sin_rows, cos_rows], axis=1)], axis=0)
    stacked_planes = jnp.concatenate([residual_value[0], residual_value[1]], axis=0)
    turned = jnp.dot(left_table.T, stacked_planes, preferred_element_type=jnp.float32).astype(jnp.bfloat16)
    joined = jnp.concatenate([turned[:PIXELS], turned[PIXELS:]], axis=1)
    right_table = jnp.concatenate([cos_cols, -sin_cols], axis=0)
    return jnp.dot(joined, right_table, preferred_element_type=jnp.float32)


def reference(sky_model, beam, tile_anchor, coverage, unit_chan, unit_block, unit_occupied_mask, observed):
    def unit_step(drawing_board, flat_unit):
        pointing_direction = flat_unit // N_SKY
        tile_keeper = flat_unit % N_SKY
        channel = unit_chan[pointing_direction, tile_keeper]
        block_first = unit_block[pointing_direction, tile_keeper, 0]
        block_second = unit_block[pointing_direction, tile_keeper, 1]
        unit_presence = unit_occupied_mask[pointing_direction, tile_keeper]

        def tables_for(slot_index):
            target = coverage[pointing_direction, slot_index]
            tables = phase_tables(block_first, tile_anchor[target, 0]) + phase_tables(block_second, tile_anchor[target, 1])
            return target, tables

        def forward_slot_entry(slot_index, model_total_sum):
            target, tables = tables_for(slot_index)
            weighted = apply_beam(sky_model[target], beam[pointing_direction, channel, slot_index])
            return model_total_sum + predict(weighted, tables)

        empty_sky_model = jnp.zeros((2, PIXELS, PIXELS), jnp.float32)
        model_total_sum = lax.cond(unit_presence > 0, lambda: lax.fori_loop(0, N_SKY, forward_slot_entry, empty_sky_model), lambda: empty_sky_model)
        residual_value = ((observed[pointing_direction, tile_keeper].astype(jnp.float32) - model_total_sum) * unit_presence.astype(jnp.float32)).astype(jnp.bfloat16)

        def adjoint_slot_entry(slot_index, picture):
            target, tables = tables_for(slot_index)
            profiles = beam[pointing_direction, channel, slot_index]
            gridded = regrid(residual_value, tables) * (profiles[0][:, None] * profiles[1][None, :])
            current = lax.dynamic_index_in_dim(picture, target, 0, keepdims=False)
            return lax.dynamic_update_index_in_dim(picture, current + gridded, target, 0)

        drawing_board = lax.cond(unit_presence > 0, lambda: lax.fori_loop(0, N_SKY, adjoint_slot_entry, drawing_board), lambda: drawing_board)
        return drawing_board, residual_value

    start_image = jnp.zeros((TILES, PIXELS, PIXELS), jnp.float32)
    drawing_board, residuals = lax.scan(unit_step, start_image, jnp.arange(POINTINGS * N_SKY, dtype=jnp.int32))
    return (residuals.reshape(POINTINGS, N_SKY, 2, PIXELS, PIXELS), drawing_board.astype(jnp.bfloat16))
```

```python
import math

import jax
import jax.numpy as jnp
import numpy as np
from jax import lax
from jax.experimental import pallas as pl
from jax.experimental.pallas import tpu as pltpu
from jax.sharding import Mesh, PartitionSpec as P

PIXELS = 256
GRID_TILES = 64
TURN = GRID_TILES * PIXELS
TILES_DEV = 4
CHIPS = 8
CORES = 2
UNITS = CHIPS * CORES
ROWS = 16
BF = jnp.bfloat16
F32 = jnp.float32

SMEM = pl.BlockSpec(memory_space=pltpu.SMEM)
VMEM = pl.BlockSpec(memory_space=pltpu.VMEM)


def dft_matrix():
    counter = np.arange(PIXELS)
    angles = 2.0 * np.pi * (counter[:, None] * counter[None, :] % PIXELS) / PIXELS
    return jnp.asarray(np.stack([np.cos(angles), np.sin(angles)]) / math.sqrt(PIXELS), BF)


def anchor_roots():
    angles = 2.0 * np.pi * np.arange(GRID_TILES) / GRID_TILES
    return jnp.asarray(np.stack([np.cos(angles), np.sin(angles)]), F32)


def dot(left, right):
    return jnp.dot(left, right, preferred_element_type=F32)


def slot_phase(coverage, anchors, blocks, roots, unit, slot):
    tile = coverage[0, slot]
    turns = blocks[0, unit, 0] * anchors[tile, 0] + blocks[0, unit, 1] * anchors[tile, 1]
    turns = lax.bitwise_and(turns, GRID_TILES - 1)
    return roots[0, turns], roots[1, turns]


def load_profiles(chans, beam, units, core, firsts, seconds):
    lines = []
    for unit in units:
        channel = chans[0, unit]
        for chip in range(CHIPS):
            pair = beam[0, channel, 2 * chip + core]
            lines.append(pair[0:1])
            seconds[len(lines) - 1 : len(lines), :] = pair[1:2]
    firsts[...] = jnp.transpose(jnp.concatenate(lines, axis=0))


def combine_kernel(
    place, coverage, chans, blocks, anchors, roots, tiles, beam, own, other, firsts, seconds
):
    sky = place[0]
    core = lax.bitwise_and(sky, 1)
    units = (sky, lax.bitwise_xor(sky, 1))
    load_profiles(chans, beam, units, core, firsts, seconds)
    phases = [
        [slot_phase(coverage, anchors, blocks, roots, unit, 2 * chip + core) for chip in range(CHIPS)]
        for unit in units
    ]

    @pl.loop(0, PIXELS // ROWS)
    def step(at):
        rows = pl.ds(pl.multiple_of(at * ROWS, ROWS), ROWS)
        first = firsts[rows, :]
        sums = [[jnp.zeros((ROWS, PIXELS), F32) for _ in range(2)] for _ in units]
        for chip in range(CHIPS):
            tile = tiles[chip, rows, :].astype(F32)
            for e in range(2):
                line = e * CHIPS + chip
                weighted = tile * seconds[line : line + 1, :] * first[:, line : line + 1]
                cosine, sine = phases[e][chip]
                sums[e][0] += cosine * weighted
                sums[e][1] += sine * weighted
        for plane in range(2):
            own[plane, rows, :] = sums[0][plane]
            other[plane, rows, :] = sums[1][plane].astype(BF)


def twiddles(offset):
    turns = lax.bitwise_and(offset * lax.broadcasted_iota(jnp.int32, (8, PIXELS), 1), TURN - 1)
    angles = turns.astype(F32) * (2.0 * math.pi / TURN)
    return jnp.cos(angles), jnp.sin(angles)


def unit_kernel(place, blocks, masks, own, arrived, observed, table, residual, turned, shift):
    sky = place[0]
    col_cos, col_sin = twiddles(blocks[0, sky, 1])
    row_cos, row_sin = twiddles(blocks[0, sky, 0])
    row_cos, row_sin = jnp.transpose(row_cos)[:, 0:1], jnp.transpose(row_sin)[:, 0:1]
    col_cos, col_sin = col_cos[0:1], col_sin[0:1]
    shift[0] = row_cos * col_cos - row_sin * col_sin
    shift[1] = row_sin * col_cos + row_cos * col_sin

    sum_re = own[0] + arrived[0].astype(F32)
    sum_im = own[1] + arrived[1].astype(F32)
    sky_re = (sum_re * shift[0] - sum_im * shift[1]).astype(BF)
    sky_im = (sum_re * shift[1] + sum_im * shift[0]).astype(BF)
    cosines, sines = table[0], table[1]
    part_re = (dot(sky_re, cosines) - dot(sky_im, sines)).astype(BF)
    part_im = (dot(sky_re, sines) + dot(sky_im, cosines)).astype(BF)
    model_re = dot(cosines, part_re) - dot(sines, part_im)
    model_im = -(dot(sines, part_re) + dot(cosines, part_im))

    occupied = masks[0, sky].astype(F32)
    res_re = (occupied * (observed[0, 0, 0].astype(F32) - model_re)).astype(BF)
    res_im = (occupied * (observed[0, 0, 1].astype(F32) - model_im)).astype(BF)
    residual[0, 0, 0] = res_re
    residual[0, 0, 1] = res_im
    part_re = (dot(cosines, res_re) - dot(sines, res_im)).astype(BF)
    part_im = (dot(sines, res_re) + dot(cosines, res_im)).astype(BF)
    back_re = dot(part_re, cosines) - dot(part_im, sines)
    back_im = dot(part_re, sines) + dot(part_im, cosines)
    turned[0, 0] = (back_re * shift[0] - back_im * shift[1]).astype(BF)
    turned[0, 1] = (back_re * shift[1] + back_im * shift[0]).astype(BF)


def spread_kernel(
    place, coverage, chans, blocks, anchors, roots, turned, beam, images, firsts, seconds
):
    sky = place[0]
    core = lax.bitwise_and(sky, 1)
    units = (sky - core, sky - core + 1)
    load_profiles(chans, beam, units, core, firsts, seconds)
    phases = [
        [slot_phase(coverage, anchors, blocks, roots, unit, 2 * chip + core) for chip in range(CHIPS)]
        for unit in units
    ]

    @pl.loop(0, PIXELS // ROWS)
    def step(at):
        rows = pl.ds(pl.multiple_of(at * ROWS, ROWS), ROWS)
        first = firsts[rows, :]
        planes = [[turned[e, plane, rows, :].astype(F32) for plane in range(2)] for e in range(2)]
        for chip in range(CHIPS):
            total = None
            for e in range(2):
                line = e * CHIPS + chip
                cosine, sine = phases[e][chip]
                part = cosine * planes[e][0] - sine * planes[e][1]
                part = part * seconds[line : line + 1, :] * first[:, line : line + 1]
                total = part if total is None else total + part
            images[chip, rows, :] = total.astype(BF)


def gather_kernel(place, coverage, parts, spread):
    sky = place[0]
    position = coverage[0, sky] - sky * TILES_DEV
    for other in range(TILES_DEV):
        spread[other] = jnp.zeros((PIXELS, PIXELS), BF)

    @pl.loop(0, PIXELS // ROWS)
    def step(at):
        rows = pl.ds(pl.multiple_of(at * ROWS, ROWS), ROWS)
        total = parts[0, rows, :].astype(F32)
        for chip in range(1, CHIPS):
            total += parts[chip, rows, :].astype(F32)
        spread[position, rows, :] = total.astype(BF)


def total_kernel(parts, repeated):
    pointings = parts.shape[0]
    total = parts[0].astype(F32)
    for p in range(1, pointings):
        total += parts[p].astype(F32)
    total = total.astype(BF)
    for p in range(pointings):
        repeated[p] = total


def shape(dims, kind):
    return jax.ShapeDtypeStruct(dims, kind)


def per_device(
    sky_model, beam, tile_anchor, coverage, unit_chan, unit_block, unit_occupied_mask, observed
):
    chip_core = lax.axis_index("chip") * CORES + lax.axis_index("core")
    place = chip_core.astype(jnp.int32).reshape(1)
    pointings = lax.axis_size("uv")
    roots = anchor_roots()
    profiles = [pltpu.VMEM((PIXELS, UNITS), F32), pltpu.VMEM((UNITS, PIXELS), F32)]

    own_position = coverage[0, chip_core] - chip_core * TILES_DEV
    own_tile = lax.dynamic_index_in_dim(sky_model, own_position, 0, keepdims=True)
    copies = jnp.broadcast_to(own_tile, (CHIPS, PIXELS, PIXELS))
    tiles = lax.all_to_all(copies, "chip", 0, 0, tiled=True)

    own, other = pl.pallas_call(
        combine_kernel,
        out_shape=(shape((2, PIXELS, PIXELS), F32), shape((2, PIXELS, PIXELS), BF)),
        in_specs=[SMEM] * 6 + [VMEM] * 2,
        out_specs=(VMEM, VMEM),
        scratch_shapes=profiles,
        name="combine",
    )(place, coverage, unit_chan, unit_block, tile_anchor, roots, tiles, beam)
    arrived = lax.ppermute(other, "core", [(0, 1), (1, 0)])

    residual, turned = pl.pallas_call(
        unit_kernel,
        out_shape=(
            shape((1, 1, 2, PIXELS, PIXELS), BF),
            shape((1, 2, PIXELS, PIXELS), BF),
        ),
        in_specs=[SMEM] * 3 + [VMEM] * 4,
        out_specs=(VMEM, VMEM),
        scratch_shapes=[pltpu.VMEM((2, PIXELS, PIXELS), F32)],
        name="unit",
    )(place, unit_block, unit_occupied_mask, own, arrived, observed, dft_matrix())
    both = lax.all_gather(turned, "core", axis=0, tiled=True)

    images = pl.pallas_call(
        spread_kernel,
        out_shape=shape((CHIPS, PIXELS, PIXELS), BF),
        in_specs=[SMEM] * 6 + [VMEM] * 2,
        out_specs=VMEM,
        scratch_shapes=profiles,
        name="spread",
    )(place, coverage, unit_chan, unit_block, tile_anchor, roots, both, beam)
    parts = lax.all_to_all(images, "chip", 0, 0, tiled=True)

    spread = pl.pallas_call(
        gather_kernel,
        out_shape=shape((TILES_DEV, PIXELS, PIXELS), BF),
        in_specs=[SMEM] * 2 + [VMEM],
        out_specs=VMEM,
        name="gather",
    )(place, coverage, parts)
    share = TILES_DEV * PIXELS // pointings
    spread = spread.reshape(pointings, share, PIXELS)
    shares = lax.all_to_all(spread, "uv", 0, 0, tiled=True)

    repeated = pl.pallas_call(
        total_kernel,
        out_shape=shape((pointings, share, PIXELS), BF),
        in_specs=[VMEM],
        out_specs=VMEM,
        name="total",
    )(shares)
    image = lax.all_to_all(repeated, "uv", 0, 0, tiled=True)
    return residual, image.reshape(TILES_DEV, PIXELS, PIXELS)


def solution(mesh):
    pointings = mesh.shape["uv"]
    fine = Mesh(mesh.devices.reshape(CHIPS, CORES, pointings), ("chip", "core", "uv"))
    sky = ("chip", "core")
    return jax.shard_map(
        per_device,
        mesh=fine,
        in_specs=(
            P(sky, None, None),
            P("uv", None, None, None, None),
            P(),
            P("uv", None),
            P("uv", None),
            P("uv", None, None),
            P("uv", None),
            P("uv", sky, None, None, None),
        ),
        out_specs=(P("uv", sky, None, None, None), P(sky, None, None)),
        check_vma=False,
    )
```

```python
import math

import jax
import jax.numpy as jnp
import numpy as np
from jax import lax
from jax.experimental import pallas as pl
from jax.experimental.pallas import tpu as pltpu
from jax.sharding import Mesh, PartitionSpec as P

PIXELS = 256
GRID_TILES = 64
TURN = GRID_TILES * PIXELS
TILES_DEV = 4
CHIPS = 8
CORES = 2
UNITS = CHIPS * CORES
ROWS = 16
BF = jnp.bfloat16
F32 = jnp.float32

LIMIT = pltpu.CompilerParams(vmem_limit_bytes=12 * 1024 * 1024)

SMEM = pl.BlockSpec(memory_space=pltpu.SMEM)
VMEM = pl.BlockSpec(memory_space=pltpu.VMEM)


def dft_matrix():
    counter = np.arange(PIXELS)
    angles = 2.0 * np.pi * (counter[:, None] * counter[None, :] % PIXELS) / PIXELS
    return jnp.asarray(np.stack([np.cos(angles), np.sin(angles)]) / math.sqrt(PIXELS), BF)


def anchor_roots():
    angles = 2.0 * np.pi * np.arange(GRID_TILES) / GRID_TILES
    return jnp.asarray(np.stack([np.cos(angles), np.sin(angles)]), F32)


def dot(left, right):
    return jnp.dot(left, right, preferred_element_type=F32)


def slot_phase(coverage, anchors, blocks, roots, unit, slot):
    tile = coverage[0, slot]
    turns = blocks[0, 0, unit] * anchors[0, tile] + blocks[0, 1, unit] * anchors[1, tile]
    turns = lax.bitwise_and(turns, GRID_TILES - 1)
    return roots[0, turns], roots[1, turns]


def load_profiles(chans, beam, units, core, firsts, seconds):
    lines = []
    for unit in units:
        channel = chans[0, unit]
        for chip in range(CHIPS):
            pair = beam[0, channel, 2 * chip + core]
            lines.append(pair[0:1])
            seconds[len(lines) - 1 : len(lines), :] = pair[1:2]
    firsts[...] = jnp.transpose(jnp.concatenate(lines, axis=0))


def copies_kernel(place, coverage, tiles, copies):
    sky = place[0]
    own = tiles[coverage[0, sky] - sky * TILES_DEV]
    for chip in range(CHIPS):
        copies[chip] = own


def combine_kernel(
    place, coverage, chans, blocks, anchors, roots, tiles, beam, own, other, firsts, seconds
):
    sky = place[0]
    core = lax.bitwise_and(sky, 1)
    units = (sky, lax.bitwise_xor(sky, 1))
    load_profiles(chans, beam, units, core, firsts, seconds)
    phases = [
        [slot_phase(coverage, anchors, blocks, roots, unit, 2 * chip + core) for chip in range(CHIPS)]
        for unit in units
    ]

    @pl.loop(0, PIXELS // ROWS)
    def step(at):
        rows = pl.ds(pl.multiple_of(at * ROWS, ROWS), ROWS)
        first = firsts[rows, :]
        sums = [[jnp.zeros((ROWS, PIXELS), F32) for _ in range(2)] for _ in units]
        for chip in range(CHIPS):
            tile = tiles[chip, rows, :].astype(F32)
            for e in range(2):
                line = e * CHIPS + chip
                weighted = tile * seconds[line : line + 1, :] * first[:, line : line + 1]
                cosine, sine = phases[e][chip]
                sums[e][0] += cosine * weighted
                sums[e][1] += sine * weighted
        for plane in range(2):
            own[plane, rows, :] = sums[0][plane]
            other[plane, rows, :] = sums[1][plane].astype(BF)


def twiddles(offset):
    turns = lax.bitwise_and(offset * lax.broadcasted_iota(jnp.int32, (8, PIXELS), 1), TURN - 1)
    angles = turns.astype(F32) * (2.0 * math.pi / TURN)
    return jnp.cos(angles), jnp.sin(angles)


def unit_kernel(place, blocks, masks, own, arrived, observed, table, residual, turned, shift):
    sky = place[0]
    col_cos, col_sin = twiddles(blocks[0, 1, sky])
    row_cos, row_sin = twiddles(blocks[0, 0, sky])
    row_cos, row_sin = jnp.transpose(row_cos)[:, 0:1], jnp.transpose(row_sin)[:, 0:1]
    col_cos, col_sin = col_cos[0:1], col_sin[0:1]
    shift[0] = row_cos * col_cos - row_sin * col_sin
    shift[1] = row_sin * col_cos + row_cos * col_sin

    sum_re = own[0] + arrived[0].astype(F32)
    sum_im = own[1] + arrived[1].astype(F32)
    sky_re = (sum_re * shift[0] - sum_im * shift[1]).astype(BF)
    sky_im = (sum_re * shift[1] + sum_im * shift[0]).astype(BF)
    cosines, sines = table[0], table[1]
    part_re = (dot(sky_re, cosines) - dot(sky_im, sines)).astype(BF)
    part_im = (dot(sky_re, sines) + dot(sky_im, cosines)).astype(BF)
    model_re = dot(cosines, part_re) - dot(sines, part_im)
    model_im = -(dot(sines, part_re) + dot(cosines, part_im))

    occupied = masks[0, sky].astype(F32)
    res_re = (occupied * (observed[0, 0, 0].astype(F32) - model_re)).astype(BF)
    res_im = (occupied * (observed[0, 0, 1].astype(F32) - model_im)).astype(BF)
    residual[0, 0, 0] = res_re
    residual[0, 0, 1] = res_im
    part_re = (dot(cosines, res_re) - dot(sines, res_im)).astype(BF)
    part_im = (dot(sines, res_re) + dot(cosines, res_im)).astype(BF)
    back_re = dot(part_re, cosines) - dot(part_im, sines)
    back_im = dot(part_re, sines) + dot(part_im, cosines)
    turned[0, 0] = (back_re * shift[0] - back_im * shift[1]).astype(BF)
    turned[0, 1] = (back_re * shift[1] + back_im * shift[0]).astype(BF)


def spread_kernel(
    place, coverage, chans, blocks, anchors, roots, turned, beam, images, firsts, seconds
):
    sky = place[0]
    core = lax.bitwise_and(sky, 1)
    units = (sky - core, sky - core + 1)
    load_profiles(chans, beam, units, core, firsts, seconds)
    phases = [
        [slot_phase(coverage, anchors, blocks, roots, unit, 2 * chip + core) for chip in range(CHIPS)]
        for unit in units
    ]

    @pl.loop(0, PIXELS // ROWS)
    def step(at):
        rows = pl.ds(pl.multiple_of(at * ROWS, ROWS), ROWS)
        first = firsts[rows, :]
        planes = [[turned[e, plane, rows, :].astype(F32) for plane in range(2)] for e in range(2)]
        for chip in range(CHIPS):
            total = None
            for e in range(2):
                line = e * CHIPS + chip
                cosine, sine = phases[e][chip]
                part = cosine * planes[e][0] - sine * planes[e][1]
                part = part * seconds[line : line + 1, :] * first[:, line : line + 1]
                total = part if total is None else total + part
            images[chip, rows, :] = total.astype(BF)


def gather_kernel(place, coverage, parts, spread):
    sky = place[0]
    position = coverage[0, sky] - sky * TILES_DEV
    for other in range(TILES_DEV):
        spread[other] = jnp.zeros((PIXELS, PIXELS), BF)

    @pl.loop(0, PIXELS // ROWS)
    def step(at):
        rows = pl.ds(pl.multiple_of(at * ROWS, ROWS), ROWS)
        total = parts[0, rows, :].astype(F32)
        for chip in range(1, CHIPS):
            total += parts[chip, rows, :].astype(F32)
        spread[position, rows, :] = total.astype(BF)


def total_kernel(parts, repeated):
    pointings = parts.shape[0]
    total = parts[0].astype(F32)
    for p in range(1, pointings):
        total += parts[p].astype(F32)
    total = total.astype(BF)
    for p in range(pointings):
        repeated[p] = total


def shape(dims, kind):
    return jax.ShapeDtypeStruct(dims, kind)


def per_device(
    sky_model, beam, tile_anchor, coverage, unit_chan, unit_block, unit_occupied_mask, observed
):
    chip_core = lax.axis_index("chip") * CORES + lax.axis_index("core")
    place = chip_core.astype(jnp.int32).reshape(1)
    pointings = lax.axis_size("uv")
    roots = anchor_roots()
    profiles = [pltpu.VMEM((PIXELS, UNITS), F32), pltpu.VMEM((UNITS, PIXELS), F32)]

    anchors = tile_anchor.T
    blocks = jnp.swapaxes(unit_block, 1, 2)

    copies = pl.pallas_call(
        copies_kernel,
        out_shape=shape((CHIPS, PIXELS, PIXELS), BF),
        in_specs=[SMEM] * 2 + [VMEM],
        out_specs=VMEM,
        compiler_params=LIMIT,
        name="copies",
    )(place, coverage, sky_model)
    tiles = lax.all_to_all(copies, "chip", 0, 0, tiled=True)

    own, other = pl.pallas_call(
        combine_kernel,
        out_shape=(shape((2, PIXELS, PIXELS), F32), shape((2, PIXELS, PIXELS), BF)),
        in_specs=[SMEM] * 6 + [VMEM] * 2,
        out_specs=(VMEM, VMEM),
        scratch_shapes=profiles,
        compiler_params=LIMIT,
        name="combine",
    )(place, coverage, unit_chan, blocks, anchors, roots, tiles, beam)
    arrived = lax.ppermute(other, "core", [(0, 1), (1, 0)])

    residual, turned = pl.pallas_call(
        unit_kernel,
        out_shape=(
            shape((1, 1, 2, PIXELS, PIXELS), BF),
            shape((1, 2, PIXELS, PIXELS), BF),
        ),
        in_specs=[SMEM] * 3 + [VMEM] * 4,
        out_specs=(VMEM, VMEM),
        scratch_shapes=[pltpu.VMEM((2, PIXELS, PIXELS), F32)],
        compiler_params=LIMIT,
        name="unit",
    )(place, blocks, unit_occupied_mask, own, arrived, observed, dft_matrix())
    both = lax.all_gather(turned, "core", axis=0, tiled=True)

    images = pl.pallas_call(
        spread_kernel,
        out_shape=shape((CHIPS, PIXELS, PIXELS), BF),
        in_specs=[SMEM] * 6 + [VMEM] * 2,
        out_specs=VMEM,
        scratch_shapes=profiles,
        compiler_params=LIMIT,
        name="spread",
    )(place, coverage, unit_chan, blocks, anchors, roots, both, beam)
    parts = lax.all_to_all(images, "chip", 0, 0, tiled=True)

    spread = pl.pallas_call(
        gather_kernel,
        out_shape=shape((TILES_DEV, PIXELS, PIXELS), BF),
        in_specs=[SMEM] * 2 + [VMEM],
        out_specs=VMEM,
        compiler_params=LIMIT,
        name="gather",
    )(place, coverage, parts)
    share = TILES_DEV * PIXELS // pointings
    spread = spread.reshape(pointings, share, PIXELS)
    shares = lax.all_to_all(spread, "uv", 0, 0, tiled=True)

    repeated = pl.pallas_call(
        total_kernel,
        out_shape=shape((pointings, share, PIXELS), BF),
        in_specs=[VMEM],
        out_specs=VMEM,
        compiler_params=LIMIT,
        name="total",
    )(shares)
    image = lax.all_to_all(repeated, "uv", 0, 0, tiled=True)
    return residual, image.reshape(TILES_DEV, PIXELS, PIXELS)


def solution(mesh):
    pointings = mesh.shape["uv"]
    fine = Mesh(mesh.devices.reshape(CHIPS, CORES, pointings), ("chip", "core", "uv"))
    sky = ("chip", "core")
    return jax.shard_map(
        per_device,
        mesh=fine,
        in_specs=(
            P(sky, None, None),
            P("uv", None, None, None, None),
            P(),
            P("uv", None),
            P("uv", None),
            P("uv", None, None),
            P("uv", None),
            P("uv", sky, None, None, None),
        ),
        out_specs=(P("uv", sky, None, None, None), P(sky, None, None)),
        check_vma=False,
    )
```

```python
import math

import jax
import jax.numpy as jnp
import numpy as np
from jax import lax
from jax.experimental import pallas as pl
from jax.experimental.pallas import tpu as pltpu
from jax.sharding import Mesh, PartitionSpec as P

PIXELS = 256
GRID_TILES = 64
TURN = GRID_TILES * PIXELS
TILES_DEV = 4
CHIPS = 8
CORES = 2
UNITS = CHIPS * CORES
ROWS = 16
MARK = 128
BF = jnp.bfloat16
F32 = jnp.float32

LIMIT = pltpu.CompilerParams(vmem_limit_bytes=12 * 1024 * 1024)

SMEM = pl.BlockSpec(memory_space=pltpu.SMEM)
VMEM = pl.BlockSpec(memory_space=pltpu.VMEM)


def dft_matrix():
    counter = np.arange(PIXELS)
    angles = 2.0 * np.pi * (counter[:, None] * counter[None, :] % PIXELS) / PIXELS
    return jnp.asarray(np.stack([np.cos(angles), np.sin(angles)]) / math.sqrt(PIXELS), BF)


def anchor_roots():
    angles = 2.0 * np.pi * np.arange(GRID_TILES) / GRID_TILES
    return jnp.asarray(np.stack([np.cos(angles), np.sin(angles)]), F32)


def dot(left, right):
    return jnp.dot(left, right, preferred_element_type=F32)


def slot_phase(coverage, anchors, blocks, roots, unit, slot):
    tile = coverage[0, slot]
    turns = blocks[0, 0, unit] * anchors[0, tile] + blocks[0, 1, unit] * anchors[1, tile]
    turns = lax.bitwise_and(turns, GRID_TILES - 1)
    return roots[0, turns], roots[1, turns]


def prepare_kernel(
    place, coverage, chans, blocks, anchors, roots, tiles, beam, copies, firsts, seconds, phases
):
    sky = place[0]
    own = tiles[coverage[0, sky] - sky * TILES_DEV]
    for chip in range(CHIPS):
        copies[chip] = own
    core = lax.bitwise_and(sky, 1)
    lines = []
    for e in range(CORES):
        unit = sky - core + e
        channel = chans[0, unit]
        for chip in range(CHIPS):
            line = e * CHIPS + chip
            slot = CORES * chip + core
            pair = beam[0, channel, slot]
            lines.append(pair[0:1])
            seconds[line : line + 1, :] = pair[1:2]
            cosine, sine = slot_phase(coverage, anchors, blocks, roots, unit, slot)
            phases[0, line] = cosine
            phases[1, line] = sine
    firsts[...] = jnp.transpose(jnp.concatenate(lines, axis=0))


def combine_kernel(place, phases, tiles, firsts, seconds, own, other):
    core = lax.bitwise_and(place[0], 1)

    @pl.loop(0, PIXELS // ROWS)
    def step(at):
        rows = pl.ds(pl.multiple_of(at * ROWS, ROWS), ROWS)
        first = firsts[rows, :]
        sums = [[jnp.zeros((ROWS, PIXELS), F32) for _ in range(2)] for _ in range(CORES)]
        for chip in range(CHIPS):
            tile = tiles[chip, rows, :].astype(F32)
            for e in range(CORES):
                line = e * CHIPS + chip
                weighted = tile * seconds[line : line + 1, :] * first[:, line : line + 1]
                sums[e][0] += phases[0, line] * weighted
                sums[e][1] += phases[1, line] * weighted
        for plane in range(2):
            own[plane, rows, :] = jnp.where(core == 0, sums[0][plane], sums[1][plane])
            other[0, plane, rows, :] = jnp.where(core == 0, sums[1][plane], sums[0][plane]).astype(BF)


def twiddles(offset):
    turns = lax.bitwise_and(offset * lax.broadcasted_iota(jnp.int32, (8, PIXELS), 1), TURN - 1)
    angles = turns.astype(F32) * (2.0 * math.pi / TURN)
    return jnp.cos(angles), jnp.sin(angles)


def unit_kernel(place, blocks, masks, own, arrived, observed, table, residual, turned, shift):
    sky = place[0]
    partner = 1 - lax.bitwise_and(sky, 1)
    col_cos, col_sin = twiddles(blocks[0, 1, sky])
    row_cos, row_sin = twiddles(blocks[0, 0, sky])
    row_cos, row_sin = jnp.transpose(row_cos)[:, 0:1], jnp.transpose(row_sin)[:, 0:1]
    col_cos, col_sin = col_cos[0:1], col_sin[0:1]
    shift[0] = row_cos * col_cos - row_sin * col_sin
    shift[1] = row_sin * col_cos + row_cos * col_sin

    sum_re = own[0] + arrived[partner, 0].astype(F32)
    sum_im = own[1] + arrived[partner, 1].astype(F32)
    sky_re = (sum_re * shift[0] - sum_im * shift[1]).astype(BF)
    sky_im = (sum_re * shift[1] + sum_im * shift[0]).astype(BF)
    cosines, sines = table[0], table[1]
    part_re = (dot(sky_re, cosines) - dot(sky_im, sines)).astype(BF)
    part_im = (dot(sky_re, sines) + dot(sky_im, cosines)).astype(BF)
    model_re = dot(cosines, part_re) - dot(sines, part_im)
    model_im = -(dot(sines, part_re) + dot(cosines, part_im))

    occupied = masks[0, sky].astype(F32)
    res_re = (occupied * (observed[0, 0, 0].astype(F32) - model_re)).astype(BF)
    res_im = (occupied * (observed[0, 0, 1].astype(F32) - model_im)).astype(BF)
    residual[0, 0, 0] = res_re
    residual[0, 0, 1] = res_im
    part_re = (dot(cosines, res_re) - dot(sines, res_im)).astype(BF)
    part_im = (dot(sines, res_re) + dot(cosines, res_im)).astype(BF)
    back_re = dot(part_re, cosines) - dot(part_im, sines)
    back_im = dot(part_re, sines) + dot(part_im, cosines)
    turned[0, 0] = (back_re * shift[0] - back_im * shift[1]).astype(BF)
    turned[0, 1] = (back_re * shift[1] + back_im * shift[0]).astype(BF)


def spread_kernel(phases, turned, firsts, seconds, images):
    @pl.loop(0, PIXELS // ROWS)
    def step(at):
        rows = pl.ds(pl.multiple_of(at * ROWS, ROWS), ROWS)
        first = firsts[rows, :]
        planes = [[turned[e, plane, rows, :].astype(F32) for plane in range(2)] for e in range(CORES)]
        for chip in range(CHIPS):
            total = None
            for e in range(CORES):
                line = e * CHIPS + chip
                part = phases[0, line] * planes[e][0] - phases[1, line] * planes[e][1]
                part = part * seconds[line : line + 1, :] * first[:, line : line + 1]
                total = part if total is None else total + part
            images[chip, rows, :] = total.astype(BF)


def gather_kernel(place, coverage, parts, shares):
    sky = place[0]
    position = (coverage[0, sky] - sky * TILES_DEV).astype(F32)
    pointings, share = shares.shape[0], shares.shape[1]
    total = parts[0].astype(F32)
    for chip in range(1, CHIPS):
        total += parts[chip].astype(F32)
    shares[:, :, 0:PIXELS] = total.reshape(pointings, share, PIXELS).astype(BF)
    shares[:, :, PIXELS:] = jnp.full((pointings, share, MARK), position, F32).astype(BF)


def total_kernel(shares, repeated):
    pointings, share = shares.shape[0], shares.shape[1]
    totals = [jnp.zeros((share, PIXELS), F32) for _ in range(TILES_DEV)]
    for p in range(pointings):
        values = shares[p, :, 0:PIXELS].astype(F32)
        mark = shares[p, :, PIXELS:].astype(F32)
        mark = jnp.concatenate([mark] * (PIXELS // MARK), axis=1)
        for position in range(TILES_DEV):
            totals[position] += jnp.where(mark == position, values, 0.0)
    totals = [total.astype(BF) for total in totals]
    for p in range(pointings):
        for position in range(TILES_DEV):
            repeated[p, position] = totals[position]


def shape(dims, kind):
    return jax.ShapeDtypeStruct(dims, kind)


def per_device(
    sky_model, beam, tile_anchor, coverage, unit_chan, unit_block, unit_occupied_mask, observed
):
    chip_core = lax.axis_index("chip") * CORES + lax.axis_index("core")
    place = chip_core.astype(jnp.int32).reshape(1)
    pointings = lax.axis_size("uv")
    anchors = tile_anchor.T
    blocks = jnp.swapaxes(unit_block, 1, 2)

    copies, firsts, seconds, phases = pl.pallas_call(
        prepare_kernel,
        out_shape=(
            shape((CHIPS, PIXELS, PIXELS), BF),
            shape((PIXELS, UNITS), F32),
            shape((UNITS, PIXELS), F32),
            shape((2, UNITS), F32),
        ),
        in_specs=[SMEM] * 6 + [VMEM] * 2,
        out_specs=(VMEM, VMEM, VMEM, SMEM),
        compiler_params=LIMIT,
        name="prepare",
    )(place, coverage, unit_chan, blocks, anchors, anchor_roots(), sky_model, beam)
    tiles = lax.all_to_all(copies, "chip", 0, 0, tiled=True)

    own, other = pl.pallas_call(
        combine_kernel,
        out_shape=(shape((2, PIXELS, PIXELS), F32), shape((1, 2, PIXELS, PIXELS), BF)),
        in_specs=[SMEM] * 2 + [VMEM] * 3,
        out_specs=(VMEM, VMEM),
        compiler_params=LIMIT,
        name="combine",
    )(place, phases, tiles, firsts, seconds)
    arrived = lax.all_gather(other, "core", axis=0, tiled=True)

    residual, turned = pl.pallas_call(
        unit_kernel,
        out_shape=(
            shape((1, 1, 2, PIXELS, PIXELS), BF),
            shape((1, 2, PIXELS, PIXELS), BF),
        ),
        in_specs=[SMEM] * 3 + [VMEM] * 4,
        out_specs=(VMEM, VMEM),
        scratch_shapes=[pltpu.VMEM((2, PIXELS, PIXELS), F32)],
        compiler_params=LIMIT,
        name="unit",
    )(place, blocks, unit_occupied_mask, own, arrived, observed, dft_matrix())
    both = lax.all_gather(turned, "core", axis=0, tiled=True)

    images = pl.pallas_call(
        spread_kernel,
        out_shape=shape((CHIPS, PIXELS, PIXELS), BF),
        in_specs=[SMEM] + [VMEM] * 3,
        out_specs=VMEM,
        compiler_params=LIMIT,
        name="spread",
    )(phases, both, firsts, seconds)
    parts = lax.all_to_all(images, "chip", 0, 0, tiled=True)

    share = PIXELS // pointings
    shares = pl.pallas_call(
        gather_kernel,
        out_shape=shape((pointings, share, PIXELS + MARK), BF),
        in_specs=[SMEM] * 2 + [VMEM],
        out_specs=VMEM,
        compiler_params=LIMIT,
        name="gather",
    )(place, coverage, parts)
    shares = lax.all_to_all(shares, "uv", 0, 0, tiled=True)

    repeated = pl.pallas_call(
        total_kernel,
        out_shape=shape((pointings, TILES_DEV, share, PIXELS), BF),
        in_specs=[VMEM],
        out_specs=VMEM,
        compiler_params=LIMIT,
        name="total",
    )(shares)
    image = lax.all_to_all(repeated, "uv", 0, 0, tiled=True)
    return residual, jnp.swapaxes(image, 0, 1).reshape(TILES_DEV, PIXELS, PIXELS)


def solution(mesh):
    pointings = mesh.shape["uv"]
    fine = Mesh(mesh.devices.reshape(CHIPS, CORES, pointings), ("chip", "core", "uv"))
    sky = ("chip", "core")
    return jax.shard_map(
        per_device,
        mesh=fine,
        in_specs=(
            P(sky, None, None),
            P("uv", None, None, None, None),
            P(),
            P("uv", None),
            P("uv", None),
            P("uv", None, None),
            P("uv", None),
            P("uv", sky, None, None, None),
        ),
        out_specs=(P("uv", sky, None, None, None), P(sky, None, None)),
        check_vma=False,
    )
```

```python
import math

import jax
import jax.numpy as jnp
import numpy as np
from jax import lax
from jax.experimental import pallas as pl
from jax.experimental.pallas import tpu as pltpu
from jax.sharding import Mesh, PartitionSpec as P

PIXELS = 256
GRID_TILES = 64
TURN = GRID_TILES * PIXELS
TILES_DEV = 4
CHIPS = 8
CORES = 2
UNITS = CHIPS * CORES
ROWS = 32
UNROLL = 2
MARK = 128
COSINE = UNITS
SINE = UNITS + 8
LINES = UNITS + 16
BF = jnp.bfloat16
F32 = jnp.float32

LIMIT = pltpu.CompilerParams(vmem_limit_bytes=12 * 1024 * 1024)

SMEM = pl.BlockSpec(memory_space=pltpu.SMEM)
VMEM = pl.BlockSpec(memory_space=pltpu.VMEM)


def dft_matrix():
    counter = np.arange(PIXELS)
    angles = 2.0 * np.pi * (counter[:, None] * counter[None, :] % PIXELS) / PIXELS
    return jnp.asarray(np.stack([np.cos(angles), np.sin(angles)]) / math.sqrt(PIXELS), BF)


def anchor_roots():
    angles = 2.0 * np.pi * np.arange(GRID_TILES) / GRID_TILES
    return jnp.asarray(np.stack([np.cos(angles), np.sin(angles)]), F32)


def dot(left, right):
    return jnp.dot(left, right, preferred_element_type=F32)


def slot_phase(coverage, anchors, blocks, roots, unit, slot):
    tile = coverage[0, slot]
    turns = blocks[0, 0, unit] * anchors[0, tile] + blocks[0, 1, unit] * anchors[1, tile]
    turns = lax.bitwise_and(turns, GRID_TILES - 1)
    return roots[0, turns], roots[1, turns]


def copies_kernel(place, coverage, tiles, copies, own, fetched, stored):
    sky = place[0]
    fetch = pltpu.make_async_copy(tiles.at[coverage[0, sky] - sky * TILES_DEV], own, fetched)
    fetch.start()
    fetch.wait()
    stores = [pltpu.make_async_copy(own, copies.at[chip], stored.at[chip]) for chip in range(CHIPS)]
    for store in stores:
        store.start()
    for store in stores:
        store.wait()


def twiddles(offset):
    turns = lax.bitwise_and(offset * lax.broadcasted_iota(jnp.int32, (8, PIXELS), 1), TURN - 1)
    angles = turns.astype(F32) * (2.0 * math.pi / TURN)
    return jnp.concatenate([jnp.cos(angles), jnp.sin(angles)], axis=0)


def prepare_kernel(
    place, coverage, chans, blocks, masks, anchors, roots, beam, firsts, seconds, phases, occupied
):
    sky = place[0]
    core = lax.bitwise_and(sky, 1)
    occupied[0] = masks[0, sky].astype(F32)
    lines = []
    for e in range(CORES):
        unit = sky - core + e
        channel = chans[0, unit]
        for chip in range(CHIPS):
            line = e * CHIPS + chip
            slot = CORES * chip + core
            pair = beam[0, channel, slot]
            lines.append(pair[0:1])
            seconds[line : line + 1, :] = pair[1:2]
            cosine, sine = slot_phase(coverage, anchors, blocks, roots, unit, slot)
            phases[0, line] = cosine
            phases[1, line] = sine
    seconds[UNITS:, :] = twiddles(blocks[0, 1, sky])
    firsts[...] = jnp.transpose(jnp.concatenate(lines + [twiddles(blocks[0, 0, sky])], axis=0))


def combine_kernel(
    place, phases, tiles, firsts, seconds, observed, table,
    own, other, weights, observed_near, table_near, near,
):
    core = lax.bitwise_and(place[0], 1)
    fetches = (
        pltpu.make_async_copy(observed, observed_near, near.at[0]),
        pltpu.make_async_copy(table, table_near, near.at[1]),
    )
    for fetch in fetches:
        fetch.start()

    @pl.loop(0, PIXELS // ROWS, unroll=UNROLL)
    def step(at):
        rows = pl.ds(pl.multiple_of(at * ROWS, ROWS), ROWS)
        first = firsts[rows, :]
        sums = [[jnp.zeros((ROWS, PIXELS), F32) for _ in range(2)] for _ in range(CORES)]
        for chip in range(CHIPS):
            tile = tiles[chip, rows, :].astype(F32)
            for e in range(CORES):
                line = e * CHIPS + chip
                shaped = first[:, line : line + 1] * seconds[line : line + 1, :]
                for plane in range(2):
                    weight = phases[plane, line] * shaped
                    weights[plane, line, rows, :] = weight
                    sums[e][plane] += tile * weight
        for plane in range(2):
            own[plane, rows, :] = jnp.where(core == 0, sums[0][plane], sums[1][plane])
            other[0, plane, rows, :] = jnp.where(core == 0, sums[1][plane], sums[0][plane]).astype(BF)

    for fetch in fetches:
        fetch.wait()


def unit_kernel(place, occupied, own, arrived, observed, table, firsts, seconds, residual, turned, shift):
    partner = 1 - lax.bitwise_and(place[0], 1)
    row_cos, row_sin = firsts[:, COSINE : COSINE + 1], firsts[:, SINE : SINE + 1]
    col_cos, col_sin = seconds[COSINE : COSINE + 1, :], seconds[SINE : SINE + 1, :]
    shift[0] = row_cos * col_cos - row_sin * col_sin
    shift[1] = row_sin * col_cos + row_cos * col_sin
    sum_re = own[0] + arrived[partner, 0].astype(F32)
    sum_im = own[1] + arrived[partner, 1].astype(F32)
    sky_re = (sum_re * shift[0] - sum_im * shift[1]).astype(BF)
    sky_im = (sum_re * shift[1] + sum_im * shift[0]).astype(BF)
    cosines, sines = table[0], table[1]
    part_re = (dot(sky_re, cosines) - dot(sky_im, sines)).astype(BF)
    part_im = (dot(sky_re, sines) + dot(sky_im, cosines)).astype(BF)
    model_re = dot(cosines, part_re) - dot(sines, part_im)
    model_im = -(dot(sines, part_re) + dot(cosines, part_im))

    res_re = (occupied[0] * (observed[0, 0, 0].astype(F32) - model_re)).astype(BF)
    res_im = (occupied[0] * (observed[0, 0, 1].astype(F32) - model_im)).astype(BF)
    residual[0, 0, 0] = res_re
    residual[0, 0, 1] = res_im
    part_re = (dot(cosines, res_re) - dot(sines, res_im)).astype(BF)
    part_im = (dot(sines, res_re) + dot(cosines, res_im)).astype(BF)
    back_re = dot(part_re, cosines) - dot(part_im, sines)
    back_im = dot(part_re, sines) + dot(part_im, cosines)
    turned[0, 0] = (back_re * shift[0] - back_im * shift[1]).astype(BF)
    turned[0, 1] = (back_re * shift[1] + back_im * shift[0]).astype(BF)


def spread_kernel(turned, weights, images):
    @pl.loop(0, PIXELS // ROWS, unroll=UNROLL)
    def step(at):
        rows = pl.ds(pl.multiple_of(at * ROWS, ROWS), ROWS)
        planes = [[turned[e, plane, rows, :].astype(F32) for plane in range(2)] for e in range(CORES)]
        for chip in range(CHIPS):
            total = None
            for e in range(CORES):
                line = e * CHIPS + chip
                part = planes[e][0] * weights[0, line, rows, :] - planes[e][1] * weights[1, line, rows, :]
                total = part if total is None else total + part
            images[chip, rows, :] = total.astype(BF)


def gather_kernel(place, coverage, parts, shares):
    sky = place[0]
    position = (coverage[0, sky] - sky * TILES_DEV).astype(F32)
    pointings, share = shares.shape[0], shares.shape[1]
    total = parts[0].astype(F32)
    for chip in range(1, CHIPS):
        total += parts[chip].astype(F32)
    shares[:, :, 0:PIXELS] = total.reshape(pointings, share, PIXELS).astype(BF)
    shares[:, :, PIXELS:] = jnp.full((pointings, share, MARK), position, F32).astype(BF)


def total_kernel(shares, repeated):
    pointings, share = shares.shape[0], shares.shape[1]
    totals = [jnp.zeros((share, PIXELS), F32) for _ in range(TILES_DEV)]
    for p in range(pointings):
        values = shares[p, :, 0:PIXELS].astype(F32)
        mark = shares[p, :, PIXELS:].astype(F32)
        mark = jnp.concatenate([mark] * (PIXELS // MARK), axis=1)
        for position in range(TILES_DEV):
            totals[position] += jnp.where(mark == position, values, 0.0)
    totals = [total.astype(BF) for total in totals]
    for p in range(pointings):
        for position in range(TILES_DEV):
            repeated[p, position] = totals[position]


def shape(dims, kind):
    return jax.ShapeDtypeStruct(dims, kind)


def per_device(
    sky_model, beam, tile_anchor, coverage, unit_chan, unit_block, unit_occupied_mask, observed
):
    chip_core = lax.axis_index("chip") * CORES + lax.axis_index("core")
    place = chip_core.astype(jnp.int32).reshape(1)
    pointings = lax.axis_size("uv")
    anchors = tile_anchor.T
    blocks = jnp.swapaxes(unit_block, 1, 2)

    copies = pl.pallas_call(
        copies_kernel,
        out_shape=shape((CHIPS, PIXELS, PIXELS), BF),
        in_specs=[SMEM] * 2 + [pl.BlockSpec(memory_space=pl.ANY)],
        out_specs=pl.BlockSpec(memory_space=pl.ANY),
        scratch_shapes=[
            pltpu.VMEM((PIXELS, PIXELS), BF),
            pltpu.SemaphoreType.DMA,
            pltpu.SemaphoreType.DMA((CHIPS,)),
        ],
        name="copies",
    )(place, coverage, sky_model)
    tiles = lax.all_to_all(copies, "chip", 0, 0, tiled=True)

    firsts, seconds, phases, occupied = pl.pallas_call(
        prepare_kernel,
        out_shape=(
            shape((PIXELS, LINES), F32),
            shape((LINES, PIXELS), F32),
            shape((2, UNITS), F32),
            shape((1,), F32),
        ),
        in_specs=[SMEM] * 7 + [VMEM],
        out_specs=(VMEM, VMEM, SMEM, SMEM),
        compiler_params=LIMIT,
        name="prepare",
    )(place, coverage, unit_chan, blocks, unit_occupied_mask, anchors, anchor_roots(), beam)

    far = pltpu.with_memory_space_constraint
    own, other, weights, observed_near, table_near = pl.pallas_call(
        combine_kernel,
        out_shape=(
            shape((2, PIXELS, PIXELS), F32),
            shape((1, 2, PIXELS, PIXELS), BF),
            shape((2, UNITS, PIXELS, PIXELS), F32),
            shape((1, 1, 2, PIXELS, PIXELS), BF),
            shape((2, PIXELS, PIXELS), BF),
        ),
        in_specs=[SMEM] * 2 + [VMEM] * 3 + [pl.BlockSpec(memory_space=pltpu.HBM)] * 2,
        out_specs=(VMEM,) * 5,
        scratch_shapes=[pltpu.SemaphoreType.DMA((2,))],
        compiler_params=LIMIT,
        name="combine",
    )(place, phases, tiles, firsts, seconds, far(observed, pltpu.HBM), far(dft_matrix(), pltpu.HBM))
    arrived = lax.all_gather(other, "core", axis=0, tiled=True)

    residual, turned = pl.pallas_call(
        unit_kernel,
        out_shape=(
            shape((1, 1, 2, PIXELS, PIXELS), BF),
            shape((1, 2, PIXELS, PIXELS), BF),
        ),
        in_specs=[SMEM] * 2 + [VMEM] * 6,
        out_specs=(VMEM, VMEM),
        scratch_shapes=[pltpu.VMEM((2, PIXELS, PIXELS), F32)],
        compiler_params=LIMIT,
        name="unit",
    )(place, occupied, own, arrived, observed_near, table_near, firsts, seconds)
    both = lax.all_gather(turned, "core", axis=0, tiled=True)

    images = pl.pallas_call(
        spread_kernel,
        out_shape=shape((CHIPS, PIXELS, PIXELS), BF),
        in_specs=[VMEM] * 2,
        out_specs=VMEM,
        compiler_params=LIMIT,
        name="spread",
    )(both, weights)
    parts = lax.all_to_all(images, "chip", 0, 0, tiled=True)

    share = PIXELS // pointings
    shares = pl.pallas_call(
        gather_kernel,
        out_shape=shape((pointings, share, PIXELS + MARK), BF),
        in_specs=[SMEM] * 2 + [VMEM],
        out_specs=VMEM,
        compiler_params=LIMIT,
        name="gather",
    )(place, coverage, parts)
    shares = lax.all_to_all(shares, "uv", 0, 0, tiled=True)

    repeated = pl.pallas_call(
        total_kernel,
        out_shape=shape((pointings, TILES_DEV, share, PIXELS), BF),
        in_specs=[VMEM],
        out_specs=VMEM,
        compiler_params=LIMIT,
        name="total",
    )(shares)
    image = lax.all_to_all(repeated, "uv", 0, 0, tiled=True)
    return residual, jnp.swapaxes(image, 0, 1).reshape(TILES_DEV, PIXELS, PIXELS)


def solution(mesh):
    pointings = mesh.shape["uv"]
    fine = Mesh(mesh.devices.reshape(CHIPS, CORES, pointings), ("chip", "core", "uv"))
    sky = ("chip", "core")
    return jax.shard_map(
        per_device,
        mesh=fine,
        in_specs=(
            P(sky, None, None),
            P("uv", None, None, None, None),
            P(),
            P("uv", None),
            P("uv", None),
            P("uv", None, None),
            P("uv", None),
            P("uv", sky, None, None, None),
        ),
        out_specs=(P("uv", sky, None, None, None), P(sky, None, None)),
        check_vma=False,
    )
```

```python
import math

import jax
import jax.numpy as jnp
import numpy as np
from jax import lax
from jax.experimental import pallas as pl
from jax.experimental.pallas import tpu as pltpu
from jax.sharding import Mesh, PartitionSpec as P

PIXELS = 256
GRID_TILES = 64
TURN = GRID_TILES * PIXELS
TILES_DEV = 4
CHIPS = 8
CORES = 2
UNITS = CHIPS * CORES
ROWS = 32
UNROLL = 2
MARK = 128
COSINE = UNITS
SINE = UNITS + 8
LINES = UNITS + 16
BF = jnp.bfloat16
F32 = jnp.float32

LIMIT = pltpu.CompilerParams(vmem_limit_bytes=12 * 1024 * 1024)

SMEM = pl.BlockSpec(memory_space=pltpu.SMEM)
VMEM = pl.BlockSpec(memory_space=pltpu.VMEM)


def dft_matrix():
    counter = np.arange(PIXELS)
    angles = 2.0 * np.pi * (counter[:, None] * counter[None, :] % PIXELS) / PIXELS
    return jnp.asarray(np.stack([np.cos(angles), np.sin(angles)]) / math.sqrt(PIXELS), BF)


def anchor_roots():
    angles = 2.0 * np.pi * np.arange(GRID_TILES) / GRID_TILES
    return jnp.asarray(np.stack([np.cos(angles), np.sin(angles)]), F32)


def sky_index():
    return lax.axis_index("chip") * CORES + lax.axis_index("core")


def dot(left, right):
    return jnp.dot(left, right, preferred_element_type=F32)


def slot_phase(coverage, anchors, blocks, roots, unit, slot):
    tile = coverage[0, slot]
    turns = blocks[0, 0, unit] * anchors[0, tile] + blocks[0, 1, unit] * anchors[1, tile]
    turns = lax.bitwise_and(turns, GRID_TILES - 1)
    return roots[0, turns], roots[1, turns]


def copies_kernel(coverage, tiles, copies, covered, near, fetched, stored):
    sky = sky_index()
    fetches = (
        pltpu.make_async_copy(coverage, covered, fetched.at[0]),
        pltpu.make_async_copy(tiles, near, fetched.at[1]),
    )
    for fetch in fetches:
        fetch.start()
    for fetch in fetches:
        fetch.wait()
    own = near.at[covered[0, sky] - sky * TILES_DEV]
    stores = [pltpu.make_async_copy(own, copies.at[chip], stored.at[chip]) for chip in range(CHIPS)]
    for store in stores:
        store.start()
    for store in stores:
        store.wait()


def twiddles(offset):
    turns = lax.bitwise_and(offset * lax.broadcasted_iota(jnp.int32, (8, PIXELS), 1), TURN - 1)
    angles = turns.astype(F32) * (2.0 * math.pi / TURN)
    return jnp.concatenate([jnp.cos(angles), jnp.sin(angles)], axis=0)


def prepare_kernel(
    place, coverage, chans, blocks, masks, anchors, roots, beam, firsts, seconds, phases, occupied
):
    sky = place[0]
    core = lax.bitwise_and(sky, 1)
    occupied[0] = masks[0, sky].astype(F32)
    lines = []
    for e in range(CORES):
        unit = sky - core + e
        channel = chans[0, unit]
        for chip in range(CHIPS):
            line = e * CHIPS + chip
            slot = CORES * chip + core
            pair = beam[0, channel, slot]
            lines.append(pair[0:1])
            seconds[line : line + 1, :] = pair[1:2]
            cosine, sine = slot_phase(coverage, anchors, blocks, roots, unit, slot)
            phases[0, line] = cosine
            phases[1, line] = sine
    seconds[UNITS:, :] = twiddles(blocks[0, 1, sky])
    firsts[...] = jnp.transpose(jnp.concatenate(lines + [twiddles(blocks[0, 0, sky])], axis=0))


def combine_kernel(
    place, phases, tiles, firsts, seconds, observed, table,
    own, other, weights, observed_near, table_near, near,
):
    core = lax.bitwise_and(place[0], 1)
    fetches = (
        pltpu.make_async_copy(observed, observed_near, near.at[0]),
        pltpu.make_async_copy(table, table_near, near.at[1]),
    )
    for fetch in fetches:
        fetch.start()

    @pl.loop(0, PIXELS // ROWS, unroll=UNROLL)
    def step(at):
        rows = pl.ds(pl.multiple_of(at * ROWS, ROWS), ROWS)
        first = firsts[rows, :]
        sums = [[jnp.zeros((ROWS, PIXELS), F32) for _ in range(2)] for _ in range(CORES)]
        for chip in range(CHIPS):
            tile = tiles[chip, rows, :].astype(F32)
            for e in range(CORES):
                line = e * CHIPS + chip
                shaped = first[:, line : line + 1] * seconds[line : line + 1, :]
                for plane in range(2):
                    weight = phases[plane, line] * shaped
                    weights[plane, line, rows, :] = weight
                    sums[e][plane] += tile * weight
        for plane in range(2):
            own[plane, rows, :] = jnp.where(core == 0, sums[0][plane], sums[1][plane])
            other[0, plane, rows, :] = jnp.where(core == 0, sums[1][plane], sums[0][plane]).astype(BF)

    for fetch in fetches:
        fetch.wait()


def unit_kernel(place, occupied, own, arrived, observed, table, firsts, seconds, residual, turned, shift):
    partner = 1 - lax.bitwise_and(place[0], 1)
    row_cos, row_sin = firsts[:, COSINE : COSINE + 1], firsts[:, SINE : SINE + 1]
    col_cos, col_sin = seconds[COSINE : COSINE + 1, :], seconds[SINE : SINE + 1, :]
    shift[0] = row_cos * col_cos - row_sin * col_sin
    shift[1] = row_sin * col_cos + row_cos * col_sin
    sum_re = own[0] + arrived[partner, 0].astype(F32)
    sum_im = own[1] + arrived[partner, 1].astype(F32)
    sky_re = (sum_re * shift[0] - sum_im * shift[1]).astype(BF)
    sky_im = (sum_re * shift[1] + sum_im * shift[0]).astype(BF)
    cosines, sines = table[0], table[1]
    real_rows = jnp.concatenate([cosines, -sines], axis=1)
    imag_rows = jnp.concatenate([sines, cosines], axis=1)
    real_cols = jnp.concatenate([cosines, -sines], axis=0)
    imag_cols = jnp.concatenate([sines, cosines], axis=0)
    sky_both = jnp.concatenate([sky_re, sky_im], axis=1)
    part = jnp.concatenate([dot(sky_both, real_cols).astype(BF), dot(sky_both, imag_cols).astype(BF)], axis=0)
    model_re = dot(real_rows, part)
    model_im = -dot(imag_rows, part)

    res_re = (occupied[0] * (observed[0, 0, 0].astype(F32) - model_re)).astype(BF)
    res_im = (occupied[0] * (observed[0, 0, 1].astype(F32) - model_im)).astype(BF)
    residual[0, 0, 0] = res_re
    residual[0, 0, 1] = res_im
    res_both = jnp.concatenate([res_re, res_im], axis=0)
    part = jnp.concatenate([dot(real_rows, res_both).astype(BF), dot(imag_rows, res_both).astype(BF)], axis=1)
    back_re = dot(part, real_cols)
    back_im = dot(part, imag_cols)
    turned[0, 0] = (back_re * shift[0] - back_im * shift[1]).astype(BF)
    turned[0, 1] = (back_re * shift[1] + back_im * shift[0]).astype(BF)


def spread_kernel(turned, weights, images):
    @pl.loop(0, PIXELS // ROWS, unroll=UNROLL)
    def step(at):
        rows = pl.ds(pl.multiple_of(at * ROWS, ROWS), ROWS)
        planes = [[turned[e, plane, rows, :].astype(F32) for plane in range(2)] for e in range(CORES)]
        for chip in range(CHIPS):
            total = None
            for e in range(CORES):
                line = e * CHIPS + chip
                part = planes[e][0] * weights[0, line, rows, :] - planes[e][1] * weights[1, line, rows, :]
                total = part if total is None else total + part
            images[chip, rows, :] = total.astype(BF)


def gather_kernel(place, coverage, parts, shares):
    sky = place[0]
    position = (coverage[0, sky] - sky * TILES_DEV).astype(F32)
    pointings, share = shares.shape[0], shares.shape[1]
    total = parts[0].astype(F32)
    for chip in range(1, CHIPS):
        total += parts[chip].astype(F32)
    shares[:, :, 0:PIXELS] = total.reshape(pointings, share, PIXELS).astype(BF)
    shares[:, :, PIXELS:] = jnp.full((pointings, share, MARK), position, F32).astype(BF)


def total_kernel(shares, repeated):
    pointings, share = shares.shape[0], shares.shape[1]
    totals = [jnp.zeros((share, PIXELS), F32) for _ in range(TILES_DEV)]
    for p in range(pointings):
        values = shares[p, :, 0:PIXELS].astype(F32)
        mark = shares[p, :, PIXELS:].astype(F32)
        mark = jnp.concatenate([mark] * (PIXELS // MARK), axis=1)
        for position in range(TILES_DEV):
            totals[position] += jnp.where(mark == position, values, 0.0)
    totals = [total.astype(BF) for total in totals]
    for p in range(pointings):
        for position in range(TILES_DEV):
            repeated[p, position] = totals[position]


def shape(dims, kind):
    return jax.ShapeDtypeStruct(dims, kind)


def per_device(
    sky_model, beam, tile_anchor, coverage, unit_chan, unit_block, unit_occupied_mask, observed
):
    place = sky_index().astype(jnp.int32).reshape(1)
    pointings = lax.axis_size("uv")
    anchors = tile_anchor.T
    blocks = jnp.swapaxes(unit_block, 1, 2)

    copies = pl.pallas_call(
        copies_kernel,
        out_shape=shape((CHIPS, PIXELS, PIXELS), BF),
        in_specs=[pl.BlockSpec(memory_space=pl.ANY)] * 2,
        out_specs=pl.BlockSpec(memory_space=pl.ANY),
        scratch_shapes=[
            pltpu.SMEM((1, UNITS), jnp.int32),
            pltpu.VMEM((TILES_DEV, PIXELS, PIXELS), BF),
            pltpu.SemaphoreType.DMA((2,)),
            pltpu.SemaphoreType.DMA((CHIPS,)),
        ],
        name="copies",
    )(coverage, sky_model)
    tiles = lax.all_to_all(copies, "chip", 0, 0, tiled=True)

    firsts, seconds, phases, occupied = pl.pallas_call(
        prepare_kernel,
        out_shape=(
            shape((PIXELS, LINES), F32),
            shape((LINES, PIXELS), F32),
            shape((2, UNITS), F32),
            shape((1,), F32),
        ),
        in_specs=[SMEM] * 7 + [VMEM],
        out_specs=(VMEM, VMEM, SMEM, SMEM),
        compiler_params=LIMIT,
        name="prepare",
    )(place, coverage, unit_chan, blocks, unit_occupied_mask, anchors, anchor_roots(), beam)

    far = pltpu.with_memory_space_constraint
    own, other, weights, observed_near, table_near = pl.pallas_call(
        combine_kernel,
        out_shape=(
            shape((2, PIXELS, PIXELS), F32),
            shape((1, 2, PIXELS, PIXELS), BF),
            shape((2, UNITS, PIXELS, PIXELS), F32),
            shape((1, 1, 2, PIXELS, PIXELS), BF),
            shape((2, PIXELS, PIXELS), BF),
        ),
        in_specs=[SMEM] * 2 + [VMEM] * 3 + [pl.BlockSpec(memory_space=pltpu.HBM)] * 2,
        out_specs=(VMEM,) * 5,
        scratch_shapes=[pltpu.SemaphoreType.DMA((2,))],
        compiler_params=LIMIT,
        name="combine",
    )(place, phases, tiles, firsts, seconds, far(observed, pltpu.HBM), far(dft_matrix(), pltpu.HBM))
    arrived = lax.all_gather(other, "core", axis=0, tiled=True)

    residual, turned = pl.pallas_call(
        unit_kernel,
        out_shape=(
            shape((1, 1, 2, PIXELS, PIXELS), BF),
            shape((1, 2, PIXELS, PIXELS), BF),
        ),
        in_specs=[SMEM] * 2 + [VMEM] * 6,
        out_specs=(VMEM, VMEM),
        scratch_shapes=[pltpu.VMEM((2, PIXELS, PIXELS), F32)],
        compiler_params=LIMIT,
        name="unit",
    )(place, occupied, own, arrived, observed_near, table_near, firsts, seconds)
    both = lax.all_gather(turned, "core", axis=0, tiled=True)

    images = pl.pallas_call(
        spread_kernel,
        out_shape=shape((CHIPS, PIXELS, PIXELS), BF),
        in_specs=[VMEM] * 2,
        out_specs=VMEM,
        compiler_params=LIMIT,
        name="spread",
    )(both, weights)
    parts = lax.all_to_all(images, "chip", 0, 0, tiled=True)

    share = PIXELS // pointings
    shares = pl.pallas_call(
        gather_kernel,
        out_shape=shape((pointings, share, PIXELS + MARK), BF),
        in_specs=[SMEM] * 2 + [VMEM],
        out_specs=VMEM,
        compiler_params=LIMIT,
        name="gather",
    )(place, coverage, parts)
    shares = lax.all_to_all(shares, "uv", 0, 0, tiled=True)

    repeated = pl.pallas_call(
        total_kernel,
        out_shape=shape((pointings, TILES_DEV, share, PIXELS), BF),
        in_specs=[VMEM],
        out_specs=VMEM,
        compiler_params=LIMIT,
        name="total",
    )(shares)
    image = lax.all_to_all(repeated, "uv", 0, 0, tiled=True)
    return residual, jnp.swapaxes(image, 0, 1).reshape(TILES_DEV, PIXELS, PIXELS)


def solution(mesh):
    pointings = mesh.shape["uv"]
    fine = Mesh(mesh.devices.reshape(CHIPS, CORES, pointings), ("chip", "core", "uv"))
    sky = ("chip", "core")
    return jax.shard_map(
        per_device,
        mesh=fine,
        in_specs=(
            P(sky, None, None),
            P("uv", None, None, None, None),
            P(),
            P("uv", None),
            P("uv", None),
            P("uv", None, None),
            P("uv", None),
            P("uv", sky, None, None, None),
        ),
        out_specs=(P("uv", sky, None, None, None), P(sky, None, None)),
        check_vma=False,
    )
```

```python
import math

import jax
import jax.numpy as jnp
import numpy as np
from jax import lax
from jax.experimental import pallas as pl
from jax.experimental.pallas import tpu as pltpu
from jax.sharding import Mesh, PartitionSpec as P

PIXELS = 256
GRID_TILES = 64
TURN = GRID_TILES * PIXELS
TILES_DEV = 4
CHIPS = 8
CORES = 2
UNITS = CHIPS * CORES
ROWS = 32
UNROLL = 2
MARK = 128
COSINE = UNITS
SINE = UNITS + 8
LINES = UNITS + 16
BF = jnp.bfloat16
F32 = jnp.float32

LIMIT = pltpu.CompilerParams(vmem_limit_bytes=12 * 1024 * 1024)

SMEM = pl.BlockSpec(memory_space=pltpu.SMEM)
VMEM = pl.BlockSpec(memory_space=pltpu.VMEM)


def dft_matrix():
    counter = np.arange(PIXELS)
    angles = 2.0 * np.pi * (counter[:, None] * counter[None, :] % PIXELS) / PIXELS
    return jnp.asarray(np.stack([np.cos(angles), np.sin(angles)]) / math.sqrt(PIXELS), BF)


def anchor_roots():
    angles = 2.0 * np.pi * np.arange(GRID_TILES) / GRID_TILES
    return jnp.asarray(np.stack([np.cos(angles), np.sin(angles)]), F32)


def sky_index():
    return lax.axis_index("chip") * CORES + lax.axis_index("core")


def uv_groups(pointings):
    groups = []
    for sky in range(UNITS):
        line = range(sky * pointings, (sky + 1) * pointings)
        groups.append(list(reversed(line)) if sky % CORES else list(line))
    return groups


def dot(left, right):
    return jnp.dot(left, right, preferred_element_type=F32)


def slot_phase(coverage, anchors, blocks, roots, unit, slot):
    tile = coverage[0, slot]
    turns = blocks[0, 0, unit] * anchors[0, tile] + blocks[0, 1, unit] * anchors[1, tile]
    turns = lax.bitwise_and(turns, GRID_TILES - 1)
    return roots[0, turns], roots[1, turns]


def copies_kernel(coverage, tiles, copies, covered, near, fetched, stored):
    sky = sky_index()
    fetches = (
        pltpu.make_async_copy(coverage, covered, fetched.at[0]),
        pltpu.make_async_copy(tiles, near, fetched.at[1]),
    )
    for fetch in fetches:
        fetch.start()
    for fetch in fetches:
        fetch.wait()
    own = near.at[covered[0, sky] - sky * TILES_DEV]
    stores = [pltpu.make_async_copy(own, copies.at[chip], stored.at[chip]) for chip in range(CHIPS)]
    for store in stores:
        store.start()
    for store in stores:
        store.wait()


def twiddles(offset):
    turns = lax.bitwise_and(offset * lax.broadcasted_iota(jnp.int32, (8, PIXELS), 1), TURN - 1)
    angles = turns.astype(F32) * (2.0 * math.pi / TURN)
    return jnp.concatenate([jnp.cos(angles), jnp.sin(angles)], axis=0)


def prepare_kernel(
    place, coverage, chans, blocks, masks, anchors, roots, beam, firsts, seconds, phases, occupied
):
    sky = place[0]
    core = lax.bitwise_and(sky, 1)
    occupied[0] = masks[0, sky].astype(F32)
    lines = []
    for e in range(CORES):
        unit = sky - core + e
        channel = chans[0, unit]
        for chip in range(CHIPS):
            line = e * CHIPS + chip
            slot = CORES * chip + core
            pair = beam[0, channel, slot]
            lines.append(pair[0:1])
            seconds[line : line + 1, :] = pair[1:2]
            cosine, sine = slot_phase(coverage, anchors, blocks, roots, unit, slot)
            phases[0, line] = cosine
            phases[1, line] = sine
    seconds[UNITS:, :] = twiddles(blocks[0, 1, sky])
    firsts[...] = jnp.transpose(jnp.concatenate(lines + [twiddles(blocks[0, 0, sky])], axis=0))


def combine_kernel(
    place, phases, tiles, firsts, seconds, observed, table,
    own, other, weights, observed_near, table_near, near,
):
    core = lax.bitwise_and(place[0], 1)
    fetches = (
        pltpu.make_async_copy(observed, observed_near, near.at[0]),
        pltpu.make_async_copy(table, table_near, near.at[1]),
    )
    for fetch in fetches:
        fetch.start()

    @pl.loop(0, PIXELS // ROWS, unroll=UNROLL)
    def step(at):
        rows = pl.ds(pl.multiple_of(at * ROWS, ROWS), ROWS)
        first = firsts[rows, :]
        sums = [[jnp.zeros((ROWS, PIXELS), F32) for _ in range(2)] for _ in range(CORES)]
        for chip in range(CHIPS):
            tile = tiles[chip, rows, :].astype(F32)
            for e in range(CORES):
                line = e * CHIPS + chip
                shaped = first[:, line : line + 1] * seconds[line : line + 1, :]
                for plane in range(2):
                    weight = phases[plane, line] * shaped
                    weights[plane, line, rows, :] = weight
                    sums[e][plane] += tile * weight
        for plane in range(2):
            own[plane, rows, :] = jnp.where(core == 0, sums[0][plane], sums[1][plane])
            other[0, plane, rows, :] = jnp.where(core == 0, sums[1][plane], sums[0][plane]).astype(BF)

    for fetch in fetches:
        fetch.wait()


def unit_kernel(place, occupied, own, arrived, observed, table, firsts, seconds, residual, turned, shift):
    partner = 1 - lax.bitwise_and(place[0], 1)
    row_cos, row_sin = firsts[:, COSINE : COSINE + 1], firsts[:, SINE : SINE + 1]
    col_cos, col_sin = seconds[COSINE : COSINE + 1, :], seconds[SINE : SINE + 1, :]
    shift[0] = row_cos * col_cos - row_sin * col_sin
    shift[1] = row_sin * col_cos + row_cos * col_sin
    sum_re = own[0] + arrived[partner, 0].astype(F32)
    sum_im = own[1] + arrived[partner, 1].astype(F32)
    sky_re = (sum_re * shift[0] - sum_im * shift[1]).astype(BF)
    sky_im = (sum_re * shift[1] + sum_im * shift[0]).astype(BF)
    cosines, sines = table[0], table[1]
    real_rows = jnp.concatenate([cosines, -sines], axis=1)
    imag_rows = jnp.concatenate([sines, cosines], axis=1)
    real_cols = jnp.concatenate([cosines, -sines], axis=0)
    imag_cols = jnp.concatenate([sines, cosines], axis=0)
    sky_both = jnp.concatenate([sky_re, sky_im], axis=1)
    part = jnp.concatenate([dot(sky_both, real_cols).astype(BF), dot(sky_both, imag_cols).astype(BF)], axis=0)
    model_re = dot(real_rows, part)
    model_im = -dot(imag_rows, part)

    res_re = (occupied[0] * (observed[0, 0, 0].astype(F32) - model_re)).astype(BF)
    res_im = (occupied[0] * (observed[0, 0, 1].astype(F32) - model_im)).astype(BF)
    residual[0, 0, 0] = res_re
    residual[0, 0, 1] = res_im
    res_both = jnp.concatenate([res_re, res_im], axis=0)
    part = jnp.concatenate([dot(real_rows, res_both).astype(BF), dot(imag_rows, res_both).astype(BF)], axis=1)
    back_re = dot(part, real_cols)
    back_im = dot(part, imag_cols)
    turned[0, 0] = (back_re * shift[0] - back_im * shift[1]).astype(BF)
    turned[0, 1] = (back_re * shift[1] + back_im * shift[0]).astype(BF)


def spread_kernel(turned, weights, images):
    @pl.loop(0, PIXELS // ROWS, unroll=UNROLL)
    def step(at):
        rows = pl.ds(pl.multiple_of(at * ROWS, ROWS), ROWS)
        planes = [[turned[e, plane, rows, :].astype(F32) for plane in range(2)] for e in range(CORES)]
        for chip in range(CHIPS):
            total = None
            for e in range(CORES):
                line = e * CHIPS + chip
                part = planes[e][0] * weights[0, line, rows, :] - planes[e][1] * weights[1, line, rows, :]
                total = part if total is None else total + part
            images[chip, rows, :] = total.astype(BF)


def gather_kernel(place, coverage, parts, shares):
    sky = place[0]
    position = (coverage[0, sky] - sky * TILES_DEV).astype(F32)
    pointings, share = shares.shape[0], shares.shape[1]
    total = parts[0].astype(F32)
    for chip in range(1, CHIPS):
        total += parts[chip].astype(F32)
    shares[:, :, 0:PIXELS] = total.reshape(pointings, share, PIXELS).astype(BF)
    shares[:, :, PIXELS:] = jnp.full((pointings, share, MARK), position, F32).astype(BF)


def total_kernel(shares, repeated):
    pointings, share = shares.shape[0], shares.shape[1]
    totals = [jnp.zeros((share, PIXELS), F32) for _ in range(TILES_DEV)]
    for p in range(pointings):
        values = shares[p, :, 0:PIXELS].astype(F32)
        mark = shares[p, :, PIXELS:].astype(F32)
        mark = jnp.concatenate([mark] * (PIXELS // MARK), axis=1)
        for position in range(TILES_DEV):
            totals[position] += jnp.where(mark == position, values, 0.0)
    totals = [total.astype(BF) for total in totals]
    for p in range(pointings):
        for position in range(TILES_DEV):
            repeated[p, position] = totals[position]


def shape(dims, kind):
    return jax.ShapeDtypeStruct(dims, kind)


def per_device(
    sky_model, beam, tile_anchor, coverage, unit_chan, unit_block, unit_occupied_mask, observed
):
    place = sky_index().astype(jnp.int32).reshape(1)
    pointings = lax.axis_size("uv")
    anchors = tile_anchor.T
    blocks = jnp.swapaxes(unit_block, 1, 2)

    copies = pl.pallas_call(
        copies_kernel,
        out_shape=shape((CHIPS, PIXELS, PIXELS), BF),
        in_specs=[pl.BlockSpec(memory_space=pl.ANY)] * 2,
        out_specs=pl.BlockSpec(memory_space=pl.ANY),
        scratch_shapes=[
            pltpu.SMEM((1, UNITS), jnp.int32),
            pltpu.VMEM((TILES_DEV, PIXELS, PIXELS), BF),
            pltpu.SemaphoreType.DMA((2,)),
            pltpu.SemaphoreType.DMA((CHIPS,)),
        ],
        name="copies",
    )(coverage, sky_model)
    tiles = lax.all_to_all(copies, "chip", 0, 0, tiled=True)

    firsts, seconds, phases, occupied = pl.pallas_call(
        prepare_kernel,
        out_shape=(
            shape((PIXELS, LINES), F32),
            shape((LINES, PIXELS), F32),
            shape((2, UNITS), F32),
            shape((1,), F32),
        ),
        in_specs=[SMEM] * 7 + [VMEM],
        out_specs=(VMEM, VMEM, SMEM, SMEM),
        compiler_params=LIMIT,
        name="prepare",
    )(place, coverage, unit_chan, blocks, unit_occupied_mask, anchors, anchor_roots(), beam)

    far = pltpu.with_memory_space_constraint
    own, other, weights, observed_near, table_near = pl.pallas_call(
        combine_kernel,
        out_shape=(
            shape((2, PIXELS, PIXELS), F32),
            shape((1, 2, PIXELS, PIXELS), BF),
            shape((2, UNITS, PIXELS, PIXELS), F32),
            shape((1, 1, 2, PIXELS, PIXELS), BF),
            shape((2, PIXELS, PIXELS), BF),
        ),
        in_specs=[SMEM] * 2 + [VMEM] * 3 + [pl.BlockSpec(memory_space=pltpu.HBM)] * 2,
        out_specs=(VMEM,) * 5,
        scratch_shapes=[pltpu.SemaphoreType.DMA((2,))],
        compiler_params=LIMIT,
        name="combine",
    )(place, phases, tiles, firsts, seconds, far(observed, pltpu.HBM), far(dft_matrix(), pltpu.HBM))
    arrived = lax.all_gather(other, "core", axis=0, tiled=True)

    residual, turned = pl.pallas_call(
        unit_kernel,
        out_shape=(
            shape((1, 1, 2, PIXELS, PIXELS), BF),
            shape((1, 2, PIXELS, PIXELS), BF),
        ),
        in_specs=[SMEM] * 2 + [VMEM] * 6,
        out_specs=(VMEM, VMEM),
        scratch_shapes=[pltpu.VMEM((2, PIXELS, PIXELS), F32)],
        compiler_params=LIMIT,
        name="unit",
    )(place, occupied, own, arrived, observed_near, table_near, firsts, seconds)
    both = lax.all_gather(turned, "core", axis=0, tiled=True)

    images = pl.pallas_call(
        spread_kernel,
        out_shape=shape((CHIPS, PIXELS, PIXELS), BF),
        in_specs=[VMEM] * 2,
        out_specs=VMEM,
        compiler_params=LIMIT,
        name="spread",
    )(both, weights)
    parts = lax.all_to_all(images, "chip", 0, 0, tiled=True)

    share = PIXELS // pointings
    shares = pl.pallas_call(
        gather_kernel,
        out_shape=shape((pointings, share, PIXELS + MARK), BF),
        in_specs=[SMEM] * 2 + [VMEM],
        out_specs=VMEM,
        compiler_params=LIMIT,
        name="gather",
    )(place, coverage, parts)
    shares = lax.all_to_all(
        shares, ("chip", "core", "uv"), 0, 0, axis_index_groups=uv_groups(pointings), tiled=True
    )

    repeated = pl.pallas_call(
        total_kernel,
        out_shape=shape((pointings, TILES_DEV, share, PIXELS), BF),
        in_specs=[VMEM],
        out_specs=VMEM,
        compiler_params=LIMIT,
        name="total",
    )(shares)
    image = lax.all_to_all(
        repeated, ("chip", "core", "uv"), 0, 0, axis_index_groups=uv_groups(pointings), tiled=True
    )
    return residual, jnp.swapaxes(image, 0, 1).reshape(TILES_DEV, PIXELS, PIXELS)


def solution(mesh):
    pointings = mesh.shape["uv"]
    fine = Mesh(mesh.devices.reshape(CHIPS, CORES, pointings), ("chip", "core", "uv"))
    sky = ("chip", "core")
    return jax.shard_map(
        per_device,
        mesh=fine,
        in_specs=(
            P(sky, None, None),
            P("uv", None, None, None, None),
            P(),
            P("uv", None),
            P("uv", None),
            P("uv", None, None),
            P("uv", None),
            P("uv", sky, None, None, None),
        ),
        out_specs=(P("uv", sky, None, None, None), P(sky, None, None)),
        check_vma=False,
    )
```

```python
import math

import jax
import jax.numpy as jnp
import numpy as np
from jax import lax
from jax.experimental import pallas as pl
from jax.experimental.pallas import tpu as pltpu
from jax.sharding import Mesh, PartitionSpec as P

PIXELS = 256
GRID_TILES = 64
TURN = GRID_TILES * PIXELS
TILES_DEV = 4
CHIPS = 8
CORES = 2
UNITS = CHIPS * CORES
ROWS = 32
UNROLL = 2
BACK_ROWS = 16
BACK_UNROLL = 8
MARK = 128
COSINE = UNITS
SINE = UNITS + 8
LINES = UNITS + 16
BF = jnp.bfloat16
F32 = jnp.float32

LIMIT = pltpu.CompilerParams(vmem_limit_bytes=12 * 1024 * 1024)

SMEM = pl.BlockSpec(memory_space=pltpu.SMEM)
VMEM = pl.BlockSpec(memory_space=pltpu.VMEM)


def dft_matrix():
    counter = np.arange(PIXELS)
    angles = 2.0 * np.pi * (counter[:, None] * counter[None, :] % PIXELS) / PIXELS
    return jnp.asarray(np.stack([np.cos(angles), np.sin(angles)]) / math.sqrt(PIXELS), BF)


def anchor_roots():
    angles = 2.0 * np.pi * np.arange(GRID_TILES) / GRID_TILES
    return jnp.asarray(np.stack([np.cos(angles), np.sin(angles)]), F32)


def sky_index():
    return lax.axis_index("chip") * CORES + lax.axis_index("core")


def uv_groups(pointings):
    groups = []
    for sky in range(UNITS):
        line = range(sky * pointings, (sky + 1) * pointings)
        groups.append(list(reversed(line)) if sky % CORES else list(line))
    return groups


def dot(left, right):
    return jnp.dot(left, right, preferred_element_type=F32)


def slot_phase(coverage, anchors, blocks, roots, unit, slot):
    tile = coverage[0, slot]
    turns = blocks[0, 0, unit] * anchors[0, tile] + blocks[0, 1, unit] * anchors[1, tile]
    turns = lax.bitwise_and(turns, GRID_TILES - 1)
    return roots[0, turns], roots[1, turns]


def copies_kernel(coverage, tiles, copies, covered, near, fetched, stored):
    sky = sky_index()
    fetches = (
        pltpu.make_async_copy(coverage, covered, fetched.at[0]),
        pltpu.make_async_copy(tiles, near, fetched.at[1]),
    )
    for fetch in fetches:
        fetch.start()
    for fetch in fetches:
        fetch.wait()
    own = near.at[covered[0, sky] - sky * TILES_DEV]
    stores = [pltpu.make_async_copy(own, copies.at[chip], stored.at[chip]) for chip in range(CHIPS)]
    for store in stores:
        store.start()
    for store in stores:
        store.wait()


def twiddles(offset):
    turns = lax.bitwise_and(offset * lax.broadcasted_iota(jnp.int32, (8, PIXELS), 1), TURN - 1)
    angles = turns.astype(F32) * (2.0 * math.pi / TURN)
    return jnp.concatenate([jnp.cos(angles), jnp.sin(angles)], axis=0)


def prepare_kernel(
    coverage, chans, blocks, masks, anchors, roots, beam, firsts, seconds, phases, occupied
):
    sky = sky_index()
    core = lax.bitwise_and(sky, 1)
    occupied[0] = masks[0, sky].astype(F32)
    lines = []
    for e in range(CORES):
        unit = sky - core + e
        channel = chans[0, unit]
        for chip in range(CHIPS):
            line = e * CHIPS + chip
            slot = CORES * chip + core
            pair = beam[0, channel, slot]
            lines.append(pair[0:1])
            seconds[line : line + 1, :] = pair[1:2]
            cosine, sine = slot_phase(coverage, anchors, blocks, roots, unit, slot)
            phases[0, line] = cosine
            phases[1, line] = sine
    seconds[UNITS:, :] = twiddles(blocks[0, 1, sky])
    firsts[...] = jnp.transpose(jnp.concatenate(lines + [twiddles(blocks[0, 0, sky])], axis=0))


def combine_kernel(
    phases, tiles, firsts, seconds, observed, table,
    own, other, weights, observed_near, table_near, near,
):
    core = lax.axis_index("core")
    fetches = (
        pltpu.make_async_copy(observed, observed_near, near.at[0]),
        pltpu.make_async_copy(table, table_near, near.at[1]),
    )
    for fetch in fetches:
        fetch.start()

    @pl.loop(0, PIXELS // ROWS, unroll=UNROLL)
    def step(at):
        rows = pl.ds(pl.multiple_of(at * ROWS, ROWS), ROWS)
        first = firsts[rows, :]
        sums = [[jnp.zeros((ROWS, PIXELS), F32) for _ in range(2)] for _ in range(CORES)]
        for chip in range(CHIPS):
            tile = tiles[chip, rows, :].astype(F32)
            for e in range(CORES):
                line = e * CHIPS + chip
                shaped = first[:, line : line + 1] * seconds[line : line + 1, :]
                for plane in range(2):
                    weight = phases[plane, line] * shaped
                    weights[plane, line, rows, :] = weight
                    sums[e][plane] += tile * weight
        for plane in range(2):
            own[plane, rows, :] = jnp.where(core == 0, sums[0][plane], sums[1][plane])
            other[0, plane, rows, :] = jnp.where(core == 0, sums[1][plane], sums[0][plane]).astype(BF)

    for fetch in fetches:
        fetch.wait()


def unit_kernel(occupied, own, arrived, observed, table, firsts, seconds, residual, turned, shift):
    partner = 1 - lax.axis_index("core")
    row_cos, row_sin = firsts[:, COSINE : COSINE + 1], firsts[:, SINE : SINE + 1]
    col_cos, col_sin = seconds[COSINE : COSINE + 1, :], seconds[SINE : SINE + 1, :]
    shift[0] = row_cos * col_cos - row_sin * col_sin
    shift[1] = row_sin * col_cos + row_cos * col_sin
    sum_re = own[0] + arrived[partner, 0].astype(F32)
    sum_im = own[1] + arrived[partner, 1].astype(F32)
    sky_re = (sum_re * shift[0] - sum_im * shift[1]).astype(BF)
    sky_im = (sum_re * shift[1] + sum_im * shift[0]).astype(BF)
    cosines, sines = table[0], table[1]
    real_rows = jnp.concatenate([cosines, -sines], axis=1)
    imag_rows = jnp.concatenate([sines, cosines], axis=1)
    real_cols = jnp.concatenate([cosines, -sines], axis=0)
    imag_cols = jnp.concatenate([sines, cosines], axis=0)
    sky_both = jnp.concatenate([sky_re, sky_im], axis=1)
    part = jnp.concatenate([dot(sky_both, real_cols).astype(BF), dot(sky_both, imag_cols).astype(BF)], axis=0)
    model_re = dot(real_rows, part)
    model_im = -dot(imag_rows, part)

    res_re = (occupied[0] * (observed[0, 0, 0].astype(F32) - model_re)).astype(BF)
    res_im = (occupied[0] * (observed[0, 0, 1].astype(F32) - model_im)).astype(BF)
    residual[0, 0, 0] = res_re
    residual[0, 0, 1] = res_im
    res_both = jnp.concatenate([res_re, res_im], axis=0)
    part = jnp.concatenate([dot(real_rows, res_both).astype(BF), dot(imag_rows, res_both).astype(BF)], axis=1)
    back_re = dot(part, real_cols)
    back_im = dot(part, imag_cols)
    turned[0, 0] = (back_re * shift[0] - back_im * shift[1]).astype(BF)
    turned[0, 1] = (back_re * shift[1] + back_im * shift[0]).astype(BF)


def spread_kernel(turned, weights, images):
    @pl.loop(0, PIXELS // BACK_ROWS, unroll=BACK_UNROLL)
    def step(at):
        rows = pl.ds(pl.multiple_of(at * BACK_ROWS, BACK_ROWS), BACK_ROWS)
        planes = [[turned[e, plane, rows, :].astype(F32) for plane in range(2)] for e in range(CORES)]
        for chip in range(CHIPS):
            total = None
            for e in range(CORES):
                line = e * CHIPS + chip
                part = planes[e][0] * weights[0, line, rows, :] - planes[e][1] * weights[1, line, rows, :]
                total = part if total is None else total + part
            images[chip, rows, :] = total.astype(BF)


def gather_kernel(coverage, parts, shares):
    sky = sky_index()
    position = (coverage[0, sky] - sky * TILES_DEV).astype(F32)
    pointings, share = shares.shape[0], shares.shape[1]
    total = parts[0].astype(F32)
    for chip in range(1, CHIPS):
        total += parts[chip].astype(F32)
    shares[:, :, 0:PIXELS] = total.reshape(pointings, share, PIXELS).astype(BF)
    shares[:, :, PIXELS:] = jnp.full((pointings, share, MARK), position, F32).astype(BF)


def total_kernel(shares, repeated):
    pointings, share = shares.shape[0], shares.shape[1]
    totals = [jnp.zeros((share, PIXELS), F32) for _ in range(TILES_DEV)]
    for p in range(pointings):
        values = shares[p, :, 0:PIXELS].astype(F32)
        mark = shares[p, :, PIXELS:].astype(F32)
        mark = jnp.concatenate([mark] * (PIXELS // MARK), axis=1)
        for position in range(TILES_DEV):
            totals[position] += jnp.where(mark == position, values, 0.0)
    totals = [total.astype(BF) for total in totals]
    for p in range(pointings):
        for position in range(TILES_DEV):
            repeated[p, position] = totals[position]


def shape(dims, kind):
    return jax.ShapeDtypeStruct(dims, kind)


def per_device(
    sky_model, beam, tile_anchor, coverage, unit_chan, unit_block, unit_occupied_mask, observed
):
    pointings = lax.axis_size("uv")
    anchors = tile_anchor.T
    blocks = jnp.swapaxes(unit_block, 1, 2)

    copies = pl.pallas_call(
        copies_kernel,
        out_shape=shape((CHIPS, PIXELS, PIXELS), BF),
        in_specs=[pl.BlockSpec(memory_space=pl.ANY)] * 2,
        out_specs=pl.BlockSpec(memory_space=pl.ANY),
        scratch_shapes=[
            pltpu.SMEM((1, UNITS), jnp.int32),
            pltpu.VMEM((TILES_DEV, PIXELS, PIXELS), BF),
            pltpu.SemaphoreType.DMA((2,)),
            pltpu.SemaphoreType.DMA((CHIPS,)),
        ],
        name="copies",
    )(coverage, sky_model)
    tiles = lax.all_to_all(copies, "chip", 0, 0, tiled=True)

    firsts, seconds, phases, occupied = pl.pallas_call(
        prepare_kernel,
        out_shape=(
            shape((PIXELS, LINES), F32),
            shape((LINES, PIXELS), F32),
            shape((2, UNITS), F32),
            shape((1,), F32),
        ),
        in_specs=[SMEM] * 6 + [VMEM],
        out_specs=(VMEM, VMEM, SMEM, SMEM),
        compiler_params=LIMIT,
        name="prepare",
    )(coverage, unit_chan, blocks, unit_occupied_mask, anchors, anchor_roots(), beam)

    far = pltpu.with_memory_space_constraint
    own, other, weights, observed_near, table_near = pl.pallas_call(
        combine_kernel,
        out_shape=(
            shape((2, PIXELS, PIXELS), F32),
            shape((1, 2, PIXELS, PIXELS), BF),
            shape((2, UNITS, PIXELS, PIXELS), F32),
            shape((1, 1, 2, PIXELS, PIXELS), BF),
            shape((2, PIXELS, PIXELS), BF),
        ),
        in_specs=[SMEM] + [VMEM] * 3 + [pl.BlockSpec(memory_space=pltpu.HBM)] * 2,
        out_specs=(VMEM,) * 5,
        scratch_shapes=[pltpu.SemaphoreType.DMA((2,))],
        compiler_params=LIMIT,
        name="combine",
    )(phases, tiles, firsts, seconds, far(observed, pltpu.HBM), far(dft_matrix(), pltpu.HBM))
    arrived = lax.all_gather(other, "core", axis=0, tiled=True)

    residual, turned = pl.pallas_call(
        unit_kernel,
        out_shape=(
            shape((1, 1, 2, PIXELS, PIXELS), BF),
            shape((1, 2, PIXELS, PIXELS), BF),
        ),
        in_specs=[SMEM] + [VMEM] * 6,
        out_specs=(VMEM, VMEM),
        scratch_shapes=[pltpu.VMEM((2, PIXELS, PIXELS), F32)],
        compiler_params=LIMIT,
        name="unit",
    )(occupied, own, arrived, observed_near, table_near, firsts, seconds)
    both = lax.all_gather(turned, "core", axis=0, tiled=True)

    images = pl.pallas_call(
        spread_kernel,
        out_shape=shape((CHIPS, PIXELS, PIXELS), BF),
        in_specs=[VMEM] * 2,
        out_specs=VMEM,
        compiler_params=LIMIT,
        name="spread",
    )(both, weights)
    parts = lax.all_to_all(images, "chip", 0, 0, tiled=True)

    share = PIXELS // pointings
    shares = pl.pallas_call(
        gather_kernel,
        out_shape=shape((pointings, share, PIXELS + MARK), BF),
        in_specs=[SMEM, VMEM],
        out_specs=VMEM,
        compiler_params=LIMIT,
        name="gather",
    )(coverage, parts)
    shares = lax.all_to_all(
        shares, ("chip", "core", "uv"), 0, 0, axis_index_groups=uv_groups(pointings), tiled=True
    )

    repeated = pl.pallas_call(
        total_kernel,
        out_shape=shape((pointings, TILES_DEV, share, PIXELS), BF),
        in_specs=[VMEM],
        out_specs=VMEM,
        compiler_params=LIMIT,
        name="total",
    )(shares)
    image = lax.all_to_all(
        repeated, ("chip", "core", "uv"), 0, 0, axis_index_groups=uv_groups(pointings), tiled=True
    )
    return residual, jnp.swapaxes(image, 0, 1).reshape(TILES_DEV, PIXELS, PIXELS)


def solution(mesh):
    pointings = mesh.shape["uv"]
    fine = Mesh(mesh.devices.reshape(CHIPS, CORES, pointings), ("chip", "core", "uv"))
    sky = ("chip", "core")
    return jax.shard_map(
        per_device,
        mesh=fine,
        in_specs=(
            P(sky, None, None),
            P("uv", None, None, None, None),
            P(),
            P("uv", None),
            P("uv", None),
            P("uv", None, None),
            P("uv", None),
            P("uv", sky, None, None, None),
        ),
        out_specs=(P("uv", sky, None, None, None), P(sky, None, None)),
        check_vma=False,
    )
```

```python
import math

import jax
import jax.numpy as jnp
import numpy as np
from jax import lax
from jax.experimental import pallas as pl
from jax.experimental.pallas import tpu as pltpu
from jax.sharding import Mesh, PartitionSpec as P

PIXELS = 256
GRID_TILES = 64
TURN = GRID_TILES * PIXELS
TILES_DEV = 4
CHIPS = 8
CORES = 2
UNITS = CHIPS * CORES
ROWS = 32
UNROLL = 2
BACK_ROWS = 16
BACK_UNROLL = 8
MARK = 128
COSINE = UNITS
SINE = UNITS + 8
LINES = UNITS + 16
BF = jnp.bfloat16
F32 = jnp.float32

LIMIT = pltpu.CompilerParams(vmem_limit_bytes=12 * 1024 * 1024)

SMEM = pl.BlockSpec(memory_space=pltpu.SMEM)
VMEM = pl.BlockSpec(memory_space=pltpu.VMEM)


def dft_matrix():
    counter = np.arange(PIXELS)
    angles = 2.0 * np.pi * (counter[:, None] * counter[None, :] % PIXELS) / PIXELS
    return jnp.asarray(np.stack([np.cos(angles), np.sin(angles)]) / math.sqrt(PIXELS), BF)


def anchor_roots():
    angles = 2.0 * np.pi * np.arange(GRID_TILES) / GRID_TILES
    return jnp.asarray(np.stack([np.cos(angles), np.sin(angles)]), F32)


def sky_index():
    return lax.axis_index("chip") * CORES + lax.axis_index("core")


def uv_groups(pointings):
    groups = []
    for sky in range(UNITS):
        line = range(sky * pointings, (sky + 1) * pointings)
        groups.append(list(reversed(line)) if sky % CORES else list(line))
    return groups


def dot(left, right):
    return jnp.dot(left, right, preferred_element_type=F32)


def slot_phase(coverage, anchors, blocks, roots, unit, slot):
    tile = coverage[0, slot]
    turns = blocks[0, 0, unit] * anchors[0, tile] + blocks[0, 1, unit] * anchors[1, tile]
    turns = lax.bitwise_and(turns, GRID_TILES - 1)
    return roots[0, turns], roots[1, turns]


def copies_kernel(coverage, tiles, copies, covered, near, fetched, stored):
    sky = sky_index()
    fetches = (
        pltpu.make_async_copy(coverage, covered, fetched.at[0]),
        pltpu.make_async_copy(tiles, near, fetched.at[1]),
    )
    for fetch in fetches:
        fetch.start()
    for fetch in fetches:
        fetch.wait()
    own = near.at[covered[0, sky] - sky * TILES_DEV]
    stores = [pltpu.make_async_copy(own, copies.at[chip], stored.at[chip]) for chip in range(CHIPS)]
    for store in stores:
        store.start()
    for store in stores:
        store.wait()


def twiddles(offset):
    turns = lax.bitwise_and(offset * lax.broadcasted_iota(jnp.int32, (8, PIXELS), 1), TURN - 1)
    angles = turns.astype(F32) * (2.0 * math.pi / TURN)
    return jnp.concatenate([jnp.cos(angles), jnp.sin(angles)], axis=0)


def prepare_kernel(
    coverage, chans, blocks, masks, anchors, roots, beam, firsts, seconds, phases, facts
):
    sky = sky_index()
    core = lax.bitwise_and(sky, 1)
    position = coverage[0, sky] - sky * TILES_DEV
    facts[0:8, :] = jnp.full((8, PIXELS), masks[0, sky].astype(F32))
    facts[8:16, :] = jnp.full((8, PIXELS), position.astype(F32))
    lines = []
    for e in range(CORES):
        unit = sky - core + e
        channel = chans[0, unit]
        for chip in range(CHIPS):
            line = e * CHIPS + chip
            slot = CORES * chip + core
            pair = beam[0, channel, slot]
            lines.append(pair[0:1])
            seconds[line : line + 1, :] = pair[1:2]
            cosine, sine = slot_phase(coverage, anchors, blocks, roots, unit, slot)
            phases[0, line] = cosine
            phases[1, line] = sine
    seconds[UNITS:, :] = twiddles(blocks[0, 1, sky])
    firsts[...] = jnp.transpose(jnp.concatenate(lines + [twiddles(blocks[0, 0, sky])], axis=0))


def combine_kernel(
    phases, tiles, firsts, seconds, observed, table,
    own, other, weights, observed_near, table_near, near,
):
    core = lax.axis_index("core")
    fetches = (
        pltpu.make_async_copy(observed, observed_near, near.at[0]),
        pltpu.make_async_copy(table, table_near, near.at[1]),
    )
    for fetch in fetches:
        fetch.start()

    @pl.loop(0, PIXELS // ROWS, unroll=UNROLL)
    def step(at):
        rows = pl.ds(pl.multiple_of(at * ROWS, ROWS), ROWS)
        first = firsts[rows, :]
        sums = [[jnp.zeros((ROWS, PIXELS), F32) for _ in range(2)] for _ in range(CORES)]
        for chip in range(CHIPS):
            tile = tiles[chip, rows, :].astype(F32)
            for e in range(CORES):
                line = e * CHIPS + chip
                shaped = first[:, line : line + 1] * seconds[line : line + 1, :]
                for plane in range(2):
                    weight = phases[plane, line] * shaped
                    weights[plane, line, rows, :] = weight
                    sums[e][plane] += tile * weight
        for plane in range(2):
            own[plane, rows, :] = jnp.where(core == 0, sums[0][plane], sums[1][plane])
            other[0, plane, rows, :] = jnp.where(core == 0, sums[1][plane], sums[0][plane]).astype(BF)

    for fetch in fetches:
        fetch.wait()


def unit_kernel(facts, own, arrived, observed, table, firsts, seconds, residual, turned, shift):
    partner = 1 - lax.axis_index("core")
    row_cos, row_sin = firsts[:, COSINE : COSINE + 1], firsts[:, SINE : SINE + 1]
    col_cos, col_sin = seconds[COSINE : COSINE + 1, :], seconds[SINE : SINE + 1, :]
    shift[0] = row_cos * col_cos - row_sin * col_sin
    shift[1] = row_sin * col_cos + row_cos * col_sin
    sum_re = own[0] + arrived[partner, 0].astype(F32)
    sum_im = own[1] + arrived[partner, 1].astype(F32)
    sky_re = (sum_re * shift[0] - sum_im * shift[1]).astype(BF)
    sky_im = (sum_re * shift[1] + sum_im * shift[0]).astype(BF)
    cosines, sines = table[0], table[1]
    real_rows = jnp.concatenate([cosines, -sines], axis=1)
    imag_rows = jnp.concatenate([sines, cosines], axis=1)
    real_cols = jnp.concatenate([cosines, -sines], axis=0)
    imag_cols = jnp.concatenate([sines, cosines], axis=0)
    sky_both = jnp.concatenate([sky_re, sky_im], axis=1)
    part = jnp.concatenate([dot(sky_both, real_cols).astype(BF), dot(sky_both, imag_cols).astype(BF)], axis=0)
    model_re = dot(real_rows, part)
    model_im = -dot(imag_rows, part)

    occupied = facts[0:1, :]
    res_re = (occupied * (observed[0, 0, 0].astype(F32) - model_re)).astype(BF)
    res_im = (occupied * (observed[0, 0, 1].astype(F32) - model_im)).astype(BF)
    residual[0, 0, 0] = res_re
    residual[0, 0, 1] = res_im
    res_both = jnp.concatenate([res_re, res_im], axis=0)
    part = jnp.concatenate([dot(real_rows, res_both).astype(BF), dot(imag_rows, res_both).astype(BF)], axis=1)
    back_re = dot(part, real_cols)
    back_im = dot(part, imag_cols)
    turned[0, 0] = (back_re * shift[0] - back_im * shift[1]).astype(BF)
    turned[0, 1] = (back_re * shift[1] + back_im * shift[0]).astype(BF)


def spread_kernel(turned, weights, images):
    @pl.loop(0, PIXELS // BACK_ROWS, unroll=BACK_UNROLL)
    def step(at):
        rows = pl.ds(pl.multiple_of(at * BACK_ROWS, BACK_ROWS), BACK_ROWS)
        planes = [[turned[e, plane, rows, :].astype(F32) for plane in range(2)] for e in range(CORES)]
        for chip in range(CHIPS):
            total = None
            for e in range(CORES):
                line = e * CHIPS + chip
                part = planes[e][0] * weights[0, line, rows, :] - planes[e][1] * weights[1, line, rows, :]
                total = part if total is None else total + part
            images[chip, rows, :] = total.astype(BF)


def gather_kernel(facts, parts, shares):
    pointings, share = shares.shape[0], shares.shape[1]
    total = parts[0].astype(F32)
    for chip in range(1, CHIPS):
        total += parts[chip].astype(F32)
    shares[:, :, 0:PIXELS] = total.reshape(pointings, share, PIXELS).astype(BF)
    mark = facts[8:9, 0:MARK].reshape(1, 1, MARK)
    shares[:, :, PIXELS:] = jnp.broadcast_to(mark, (pointings, share, MARK)).astype(BF)


def total_kernel(shares, repeated):
    pointings, share = shares.shape[0], shares.shape[1]
    totals = [jnp.zeros((share, PIXELS), F32) for _ in range(TILES_DEV)]
    for p in range(pointings):
        values = shares[p, :, 0:PIXELS].astype(F32)
        mark = shares[p, :, PIXELS:].astype(F32)
        mark = jnp.concatenate([mark] * (PIXELS // MARK), axis=1)
        for position in range(TILES_DEV):
            totals[position] += jnp.where(mark == position, values, 0.0)
    totals = [total.astype(BF) for total in totals]
    for p in range(pointings):
        for position in range(TILES_DEV):
            repeated[p, position] = totals[position]


def shape(dims, kind):
    return jax.ShapeDtypeStruct(dims, kind)


def per_device(
    sky_model, beam, tile_anchor, coverage, unit_chan, unit_block, unit_occupied_mask, observed
):
    pointings = lax.axis_size("uv")
    anchors = tile_anchor.T
    blocks = jnp.swapaxes(unit_block, 1, 2)

    copies = pl.pallas_call(
        copies_kernel,
        out_shape=shape((CHIPS, PIXELS, PIXELS), BF),
        in_specs=[pl.BlockSpec(memory_space=pl.ANY)] * 2,
        out_specs=pl.BlockSpec(memory_space=pl.ANY),
        scratch_shapes=[
            pltpu.SMEM((1, UNITS), jnp.int32),
            pltpu.VMEM((TILES_DEV, PIXELS, PIXELS), BF),
            pltpu.SemaphoreType.DMA((2,)),
            pltpu.SemaphoreType.DMA((CHIPS,)),
        ],
        name="copies",
    )(coverage, sky_model)
    tiles = lax.all_to_all(copies, "chip", 0, 0, tiled=True)

    firsts, seconds, phases, facts = pl.pallas_call(
        prepare_kernel,
        out_shape=(
            shape((PIXELS, LINES), F32),
            shape((LINES, PIXELS), F32),
            shape((2, UNITS), F32),
            shape((16, PIXELS), F32),
        ),
        in_specs=[SMEM] * 6 + [VMEM],
        out_specs=(VMEM, VMEM, SMEM, VMEM),
        compiler_params=LIMIT,
        name="prepare",
    )(coverage, unit_chan, blocks, unit_occupied_mask, anchors, anchor_roots(), beam)

    far = pltpu.with_memory_space_constraint
    own, other, weights, observed_near, table_near = pl.pallas_call(
        combine_kernel,
        out_shape=(
            shape((2, PIXELS, PIXELS), F32),
            shape((1, 2, PIXELS, PIXELS), BF),
            shape((2, UNITS, PIXELS, PIXELS), F32),
            shape((1, 1, 2, PIXELS, PIXELS), BF),
            shape((2, PIXELS, PIXELS), BF),
        ),
        in_specs=[SMEM] + [VMEM] * 3 + [pl.BlockSpec(memory_space=pltpu.HBM)] * 2,
        out_specs=(VMEM,) * 5,
        scratch_shapes=[pltpu.SemaphoreType.DMA((2,))],
        compiler_params=LIMIT,
        name="combine",
    )(phases, tiles, firsts, seconds, far(observed, pltpu.HBM), far(dft_matrix(), pltpu.HBM))
    arrived = lax.all_gather(other, "core", axis=0, tiled=True)

    residual, turned = pl.pallas_call(
        unit_kernel,
        out_shape=(
            shape((1, 1, 2, PIXELS, PIXELS), BF),
            shape((1, 2, PIXELS, PIXELS), BF),
        ),
        in_specs=[VMEM] * 7,
        out_specs=(VMEM, VMEM),
        scratch_shapes=[pltpu.VMEM((2, PIXELS, PIXELS), F32)],
        compiler_params=LIMIT,
        name="unit",
    )(facts, own, arrived, observed_near, table_near, firsts, seconds)
    both = lax.all_gather(turned, "core", axis=0, tiled=True)

    images = pl.pallas_call(
        spread_kernel,
        out_shape=shape((CHIPS, PIXELS, PIXELS), BF),
        in_specs=[VMEM] * 2,
        out_specs=VMEM,
        compiler_params=LIMIT,
        name="spread",
    )(both, weights)
    parts = lax.all_to_all(images, "chip", 0, 0, tiled=True)

    share = PIXELS // pointings
    shares = pl.pallas_call(
        gather_kernel,
        out_shape=shape((pointings, share, PIXELS + MARK), BF),
        in_specs=[VMEM] * 2,
        out_specs=VMEM,
        compiler_params=LIMIT,
        name="gather",
    )(facts, parts)
    shares = lax.all_to_all(
        shares, ("chip", "core", "uv"), 0, 0, axis_index_groups=uv_groups(pointings), tiled=True
    )

    repeated = pl.pallas_call(
        total_kernel,
        out_shape=shape((pointings, TILES_DEV, share, PIXELS), BF),
        in_specs=[VMEM],
        out_specs=VMEM,
        compiler_params=LIMIT,
        name="total",
    )(shares)
    image = lax.all_to_all(
        repeated, ("chip", "core", "uv"), 0, 0, axis_index_groups=uv_groups(pointings), tiled=True
    )
    return residual, jnp.swapaxes(image, 0, 1).reshape(TILES_DEV, PIXELS, PIXELS)


def solution(mesh):
    pointings = mesh.shape["uv"]
    fine = Mesh(mesh.devices.reshape(CHIPS, CORES, pointings), ("chip", "core", "uv"))
    sky = ("chip", "core")
    return jax.shard_map(
        per_device,
        mesh=fine,
        in_specs=(
            P(sky, None, None),
            P("uv", None, None, None, None),
            P(),
            P("uv", None),
            P("uv", None),
            P("uv", None, None),
            P("uv", None),
            P("uv", sky, None, None, None),
        ),
        out_specs=(P("uv", sky, None, None, None), P(sky, None, None)),
        check_vma=False,
    )
```
